256 devices in a mesh: depth: 32 (over x, y, core), plane: 8 (over z).
Axes of the slice: x: 4, y: 4, z: 8, core: 2. Of those that a mesh axis runs over, the one named last changes fastest.
Arguments:
- spectrum: bfloat16 [2, 1024, 32, 1024], P(None, 'depth', 'plane'), may hold values from -6 to 6
- transfer_coeffs: float32 [8, 4, 4], replicated, may hold values from -3 to 3
- transfer_index: int32 [8], replicated, may hold values from 0 to 7, each once
Outputs:
- scalar_field: float32 [1024, 32, 1024], P('depth', 'plane')
- rendered: float32 [8, 4, 32, 1024], P(None, None, 'plane', 'depth')
The draws below stay inside these ranges and needn't reach their ends.
Inputs may be any that keep to these rules, and one draw needn't show every extreme that they name: `transfer_index`: each transfer function is used by exactly one image.
All inputs are finite; a program needn't handle non-finite values.
Results may differ from the reference program's by a relative error of at most 0.0003.
Values may be sent and summed in bfloat16 or wider, within the bound.
A program may use at most 64 MiB of HBM per device.

```python
import jax
import jax.numpy as jnp
from jax import lax

NX = 1024
NZ = 1024
TFS = 8
COEFS = 4
IMAGES = 8
NY = 32


def shard_levels(own_key, extent, cuts, least, high):
    def one(position, parts):
        draws = jax.random.uniform(jax.random.fold_in(jax.random.fold_in(own_key, 6), position), (parts,), jnp.float32, least / len(cuts), high / len(cuts))
        return jnp.repeat(jnp.exp(draws), extent[position] // parts).reshape((-1,) + (1,) * (len(extent) - position - 1))

    gain = one(*cuts[0])
    for cut in cuts[1:]:
        gain = gain * one(*cut)
    return gain


def bell_draw(stream_key, shape, deviation, reach, pieces=(), kind=jnp.bfloat16):
    entries = jax.random.normal(stream_key, shape, jnp.float32) * deviation
    if len(pieces) > 0:
        entries = shard_levels(stream_key, shape, pieces, -0.22, 0.18) * entries
    return jnp.clip(entries, min=-reach, max=reach).astype(kind)


def setup_inputs(seed: int = 0) -> dict:
    keys = jax.random.split(jax.random.key(seed), 4)
    return {
        "spectrum": bell_draw(keys[0], (2, NZ, NY, NX), 1.0, 6.0, ((1, 32), (2, 8))),
        "transfer_coeffs": bell_draw(keys[1], (TFS, 4, COEFS), 0.5, 3.0, (), jnp.float32),
        "transfer_index": jax.random.permutation(keys[2], TFS).astype(jnp.int32),
    }


density = 2.0
shade_gain = 0.4
highest = lax.Precision.HIGHEST

def dft_tables(length):
    indices = jnp.arange(length, dtype=jnp.int32)
    phase_index = indices[:, None] * indices[None, :] % length
    angles = phase_index.astype(jnp.float32) * (2.0 * jnp.pi / length)
    scaling = 1.0 / jnp.sqrt(jnp.float32(length))
    return (jnp.cos(angles) * scaling, jnp.sin(angles) * scaling)

def polynomial(coeffs, values):
    result = coeffs[-1] + jnp.zeros_like(values)
    for degree in range(coeffs.shape[0] - 2, -1, -1):
        result = result * values + coeffs[degree]
    return result

def reference(spectrum, transfer_coeffs, transfer_index):
    cos_z, sin_z = dft_tables(NZ)
    cos_x, sin_x = dft_tables(NX)

    def plane_field(plane_modes):
        real_part = plane_modes[0].astype(jnp.float32)
        imag_part = plane_modes[1].astype(jnp.float32)
        g_re = jnp.dot(cos_z, real_part, precision=highest) - jnp.dot(sin_z, imag_part, precision=highest)
        g_im = jnp.dot(sin_z, real_part, precision=highest) + jnp.dot(cos_z, imag_part, precision=highest)
        return jnp.dot(g_re, cos_x, precision=highest) - jnp.dot(g_im, sin_x, precision=highest)
    per_plane = lax.map(plane_field, jnp.transpose(spectrum, (2, 0, 1, 3)))
    scalar_field = jnp.transpose(per_plane, (1, 0, 2))
    slope_cells = 0.5 * (jnp.roll(per_plane, -1, 0) - jnp.roll(per_plane, 1, 0))
    selected = transfer_coeffs[transfer_index]

    def plane_image(pair):
        values, slope_plane = pair
        lighting = 1.0 + shade_gain * jnp.tanh(slope_plane)
        per_image = []
        for which_image in range(IMAGES):
            coeffs = selected[which_image]
            optical = jax.nn.softplus(polynomial(coeffs[3], values)) * (density / NZ)
            before = jnp.cumsum(optical, axis=0) - optical
            weight = jnp.exp(-before) * -jnp.expm1(-optical) * lighting
            channels = []
            for channel in range(3):
                glow_cells = jax.nn.softplus(polynomial(coeffs[channel], values))
                channels.append(lax.optimization_barrier(jnp.sum(weight * glow_cells, axis=0)))
            channels.append(jnp.exp(-lax.optimization_barrier(jnp.sum(optical, axis=0))))
            per_image.append(jnp.stack(channels))
        return jnp.stack(per_image)
    images = lax.map(plane_image, (per_plane, slope_cells))
    return (scalar_field, jnp.transpose(images, (1, 2, 0, 3)))
```

```python
import functools
import math

import jax
import jax.numpy as jnp
import ml_dtypes
import numpy as np
from jax import lax
from jax.experimental import pallas as pl
from jax.experimental.pallas import tpu as pltpu
from jax.sharding import PartitionSpec as P

NX = 1024
NZ = 1024
density = 2.0
shade_gain = 0.4
tau_scale = density / NZ
f32 = jnp.float32
bf16 = jnp.bfloat16


def split_table(values):
    high = values.astype(ml_dtypes.bfloat16)
    low = (values - high.astype(np.float64)).astype(ml_dtypes.bfloat16)
    return np.stack([high, low])


def x_tables():
    index = np.arange(NX)
    angles = (index[:, None] * index[None, :] % NX) * (2.0 * np.pi / NX)
    return split_table(np.cos(angles) / math.sqrt(NX)), split_table(np.sin(angles) / math.sqrt(NX))


def z_tables():
    q0 = np.arange(256)
    m = np.arange(256)
    tables = []
    for r in range(4):
        angles = (q0[None, :] * (4 * m[:, None] + r) % NZ) * (2.0 * np.pi / NZ)
        tables.append(np.concatenate([np.cos(angles), -np.sin(angles)], axis=1) / math.sqrt(NZ))
    return split_table(np.stack(tables))


def split(value):
    high = lax.reduce_precision(value, 8, 7)
    return high.astype(bf16), (value - high).astype(bf16)


def dot(a, b):
    return jnp.dot(a, b, preferred_element_type=f32)


def residues(re, im):
    a, b = re[0] + re[2], im[0] + im[2]
    c, d = re[0] - re[2], im[0] - im[2]
    e, f = re[1] + re[3], im[1] + im[3]
    g, h = re[1] - re[3], im[1] - im[3]
    return [(a + e, b + f), (c - h, d + g), (a - e, b - f), (c + h, d - g)]


def lighting_kernel_part(field, before, after, r):
    lane = lax.broadcasted_iota(jnp.int32, field.shape, 1)
    up = pltpu.roll(field, 96, 1)
    down = pltpu.roll(field, 32, 1)
    after = pltpu.roll(after, (96 - 32 * r) % 128, 1) if r != 3 else after
    before = pltpu.roll(before, (-32 * r) % 128, 1) if r else before
    up = jnp.where(lane >= 96, after, up)
    down = jnp.where(lane < 32, before, down)
    return 1.0 + shade_gain * jnp.tanh(0.5 * (up - down))


def coefficients(coeff_ref, index_ref):
    row = lax.broadcasted_iota(jnp.int32, (8, 128), 0)
    result = []
    for channel in range(4):
        for n in range(4):
            value = jnp.zeros((8, 128), f32)
            for image in range(8):
                value = jnp.where(row == image, coeff_ref[index_ref[image], channel * 4 + n], value)
            result.append(value)
    return result


def softplus(coeffs, s):
    p = ((coeffs[3] * s + coeffs[2]) * s + coeffs[1]) * s + coeffs[0]
    return jnp.maximum(p, jnp.log(1.0 + jnp.exp(jnp.minimum(p, 80.0))))


def opacity(depth):
    k1, k2, k3 = tau_scale, tau_scale**2 / 2, tau_scale**3 / 6
    small = depth * (k1 - depth * (k2 - depth * k3))
    large = 1.0 - jnp.exp(depth * -tau_scale)
    return jnp.where(depth < 16.0, small, large)


def render_step(coeffs, s, light, state):
    c0, c1, c2, through, depth_sum = state
    depth = softplus(coeffs[12:16], s)
    weight = through * opacity(depth)
    through = through - weight
    weight = weight * light
    c0 = c0 + weight * softplus(coeffs[0:4], s)
    c1 = c1 + weight * softplus(coeffs[4:8], s)
    c2 = c2 + weight * softplus(coeffs[8:12], s)
    return c0, c1, c2, through, depth_sum + depth


def render_kernel(coeff_ref, index_ref, field_ref, before_ref, after_ref, out_ref, light_ref):
    @pl.loop(0, 32)
    def _(step):
        rows = pl.ds(pl.multiple_of(step * 8, 8), 8)
        for r in range(4):
            light_ref[r, rows, :] = lighting_kernel_part(
                field_ref[r, rows, :], before_ref[rows, :], after_ref[rows, :], r
            )

    coeffs = coefficients(coeff_ref, index_ref)

    def body(step, state):
        rows = pl.ds(pl.multiple_of(step * 8, 8), 8)
        for k in range(8):
            for r in range(4):
                s = jnp.broadcast_to(field_ref[r, rows, :][k : k + 1, :], (8, 128))
                light = jnp.broadcast_to(light_ref[r, rows, :][k : k + 1, :], (8, 128))
                state = render_step(coeffs, s, light, state)
        return state

    zero = jnp.zeros((8, 128), f32)
    c0, c1, c2, _, depth_sum = lax.fori_loop(0, 32, body, (zero, zero, zero, zero + 1.0, zero))
    out_ref[0] = c0
    out_ref[1] = c1
    out_ref[2] = c2
    out_ref[3] = jnp.exp(depth_sum * -tau_scale)


def render(coeffs, index, field, before, after):
    smem = pl.BlockSpec(memory_space=pltpu.SMEM)
    vmem = pl.BlockSpec(memory_space=pltpu.VMEM)
    return pl.pallas_call(
        render_kernel,
        out_shape=jax.ShapeDtypeStruct((4, 8, 128), f32),
        in_specs=[smem, smem, vmem, vmem, vmem],
        out_specs=vmem,
        scratch_shapes=[pltpu.VMEM((4, 256, 128), f32)],
    )(coeffs, index, field, before, after)


def body(cos_x, sin_x, table_z, spectrum, transfer_coeffs, transfer_index):
    rows = spectrum.reshape(2, 128, NX)
    cr, ci = rows[0], rows[1]
    h_re = dot(cr, cos_x[0]) + dot(cr, cos_x[1]) - (dot(ci, sin_x[0]) + dot(ci, sin_x[1]))
    h_im = dot(cr, sin_x[0]) + dot(cr, sin_x[1]) + (dot(ci, cos_x[0]) + dot(ci, cos_x[1]))
    h = jnp.stack([h_re, h_im]).reshape(2, 32, 4, NX)
    h = lax.all_to_all(h, "depth", split_axis=3, concat_axis=1, tiled=True)
    h = h.reshape(2, 4, 256, 128)
    field = []
    for r, (re, im) in enumerate(residues(h[0], h[1])):
        high, low = split(jnp.concatenate([re, im]))
        field.append(dot(table_z[0, r], high) + dot(table_z[0, r], low) + dot(table_z[1, r], high))
    field = jnp.stack(field)
    count = lax.axis_size("plane")
    up = [(i, (i + 1) % count) for i in range(count)]
    down = [(j, i) for i, j in up]
    last = jnp.transpose(field[:, :, 96:], (1, 0, 2)).reshape(256, 128)
    first = jnp.transpose(field[:, :, :32], (1, 0, 2)).reshape(256, 128)
    before = lax.ppermute(last, "plane", up)
    after = lax.ppermute(first, "plane", down)
    rendered = render(transfer_coeffs.reshape(8, 16), transfer_index, field, before, after)
    slabs = field.reshape(4, 32, 8, 128)
    slabs = lax.all_to_all(slabs, "depth", split_axis=1, concat_axis=1, tiled=True)
    slabs = slabs.reshape(4, 32, 8, 4, 32)
    scalar_field = jnp.transpose(slabs, (2, 0, 3, 1, 4)).reshape(32, 4, NX)
    rendered = jnp.transpose(rendered.reshape(4, 8, 4, 32), (1, 0, 2, 3))
    return scalar_field, rendered


def solution(mesh):
    cos_x, sin_x = x_tables()
    table_z = z_tables()
    mapped = jax.shard_map(
        body,
        mesh=mesh,
        in_specs=(P(), P(), P(), P(None, "depth", "plane", None), P(), P()),
        out_specs=(P("depth", "plane", None), P(None, None, "plane", "depth")),
        check_vma=False,
    )

    def run(spectrum, transfer_coeffs, transfer_index):
        return mapped(cos_x, sin_x, table_z, spectrum, transfer_coeffs, transfer_index)

    return run
```

```python
import math

import jax
import jax.numpy as jnp
import ml_dtypes
import numpy as np
from jax import lax
from jax.experimental import pallas as pl
from jax.experimental.pallas import tpu as pltpu
from jax.sharding import PartitionSpec as P

NX = 1024
NZ = 1024
density = 2.0
shade_gain = 0.4
tau_scale = density / NZ
f32 = jnp.float32
bf16 = jnp.bfloat16
MESH = pl.DeviceIdType.MESH


def split_table(values):
    high = values.astype(ml_dtypes.bfloat16)
    low = (values - high.astype(np.float64)).astype(ml_dtypes.bfloat16)
    return np.stack([high, low])


def x_table():
    index = np.arange(NX)
    angles = (index[:, None] * index[None, :] % NX) * (2.0 * np.pi / NX)
    tables = [split_table(t / math.sqrt(NX)).reshape(2, NX, 8, 128) for t in (np.cos(angles), np.sin(angles))]
    return np.ascontiguousarray(np.concatenate(tables, axis=3).transpose(2, 0, 1, 3))


def z_table():
    q0 = np.arange(256)
    m = np.arange(256)
    tables = []
    for r in range(4):
        angles = (q0[None, :] * (4 * m[:, None] + r) % NZ) * (2.0 * np.pi / NZ)
        table = np.concatenate([np.cos(angles), -np.sin(angles)], axis=1) / math.sqrt(NZ)
        tables.append(split_table(table).reshape(512, 512))
    return np.stack(tables)


def split(value):
    high = value.astype(bf16)
    return high, (value - high.astype(f32)).astype(bf16)


def dot(a, b):
    return jnp.dot(a, b, preferred_element_type=f32)


def residues(re, im):
    a, b = re[0] + re[2], im[0] + im[2]
    c, d = re[0] - re[2], im[0] - im[2]
    e, f = re[1] + re[3], im[1] + im[3]
    g, h = re[1] - re[3], im[1] - im[3]
    return [(a + e, b + f), (c - h, d + g), (a - e, b - f), (c + h, d - g)]


def lighting(field, before, after, r):
    lane = lax.broadcasted_iota(jnp.int32, field.shape, 1)
    up = pltpu.roll(field, 96, 1)
    down = pltpu.roll(field, 32, 1)
    after = pltpu.roll(after, (96 - 32 * r) % 128, 1) if r != 3 else after
    before = pltpu.roll(before, (-32 * r) % 128, 1) if r else before
    up = jnp.where(lane >= 96, after, up)
    down = jnp.where(lane < 32, before, down)
    return 1.0 + shade_gain * jnp.tanh(0.5 * (up - down))


def coefficients(coeff_ref, index_ref):
    row = lax.broadcasted_iota(jnp.int32, (8, 128), 0)
    result = []
    for channel in range(4):
        for n in range(4):
            value = jnp.zeros((8, 128), f32)
            for image in range(8):
                value = jnp.where(row == image, coeff_ref[index_ref[image], channel * 4 + n], value)
            result.append(value)
    return result


def softplus(coeffs, s):
    p = ((coeffs[3] * s + coeffs[2]) * s + coeffs[1]) * s + coeffs[0]
    return jnp.maximum(p, jnp.log(1.0 + jnp.exp(jnp.minimum(p, 80.0))))


def opacity(depth):
    k1, k2, k3 = tau_scale, tau_scale**2 / 2, tau_scale**3 / 6
    small = depth * (k1 - depth * (k2 - depth * k3))
    large = 1.0 - jnp.exp(depth * -tau_scale)
    return jnp.where(depth < 16.0, small, large)


def render_step(coeffs, s, light, state):
    c0, c1, c2, through, depth_sum = state
    depth = softplus(coeffs[12:16], s)
    weight = through * opacity(depth)
    through = through - weight
    weight = weight * light
    c0 = c0 + weight * softplus(coeffs[0:4], s)
    c1 = c1 + weight * softplus(coeffs[4:8], s)
    c2 = c2 + weight * softplus(coeffs[8:12], s)
    return c0, c1, c2, through, depth_sum + depth


def shuffle(parts, place):
    group = lax.broadcasted_iota(jnp.int32, parts[0].shape, 1) // 32
    result = None
    for g in range(4):
        shift = (32 * (g - place)) % 128
        moved = pltpu.roll(parts[g], shift, 1) if shift else parts[g]
        result = moved if result is None else jnp.where(group == g, moved, result)
    return result


def kernel(
    coeff_ref, index_ref, spectrum_ref, x_hbm, z_hbm,
    field_out, image_out,
    x_ref, z_ref, mode_ref, send_ref, recv_ref, pair_ref, field_ref, light_ref, pack_ref, halo_ref, slab_ref,
    x_sem, z_sem, send_sem, recv_sem, halo_send, halo_recv, slab_send, slab_recv,
):
    me = lax.axis_index("depth")
    plane = lax.axis_index("plane")
    planes = lax.axis_size("plane")
    next_plane = lax.rem(plane + 1, planes)
    last_plane = lax.rem(plane + planes - 1, planes)

    def chunk_of(step):
        return lax.rem(me // 4 + step, 8)

    def x_copy(step):
        chunk = chunk_of(step)
        return pltpu.make_async_copy(x_hbm.at[chunk], x_ref.at[chunk], x_sem.at[step])

    z_copy = pltpu.make_async_copy(z_hbm, z_ref, z_sem)

    @pl.loop(0, 8)
    def _(step):
        x_copy(step).start()

    z_copy.start()

    barrier = pltpu.get_barrier_semaphore()

    @pl.loop(1, 32)
    def _(step):
        pl.semaphore_signal(barrier, inc=1, device_id={"depth": lax.rem(me + step, 32)}, device_id_type=MESH)

    pl.semaphore_signal(barrier, inc=1, device_id={"plane": next_plane}, device_id_type=MESH)
    pl.semaphore_signal(barrier, inc=1, device_id={"plane": last_plane}, device_id_type=MESH)

    def mode_send(to):
        return pltpu.make_async_remote_copy(
            src_ref=send_ref.at[to], dst_ref=recv_ref.at[me], send_sem=send_sem.at[to], recv_sem=recv_sem.at[me],
            device_id={"depth": to}, device_id_type=MESH,
        )

    def mode_recv(source):
        return pltpu.make_async_remote_copy(
            src_ref=send_ref.at[source], dst_ref=recv_ref.at[source], send_sem=send_sem.at[source],
            recv_sem=recv_sem.at[source], device_id={"depth": source}, device_id_type=MESH,
        )

    def mode_keep():
        return pltpu.make_async_copy(send_ref.at[me], recv_ref.at[me], recv_sem.at[me])

    @pl.loop(0, 8)
    def _(step):
        chunk = chunk_of(step)
        x_copy(step).wait()
        modes = spectrum_ref[...]
        waves = dot(modes, x_ref[chunk, 0]) + dot(modes, x_ref[chunk, 1])
        mode_ref[0] = waves[:128, :128] - waves[128:, 128:]
        mode_ref[1] = waves[:128, 128:] + waves[128:, :128]
        for part in range(2):
            rows = [mode_ref[part, pl.ds(y, 32, stride=4), :] for y in range(4)]
            for d in range(4):
                send_ref[chunk * 4 + d, part] = shuffle(rows, d)

        @pl.when(step == 0)
        def _():
            pl.semaphore_wait(barrier, 33)

        @pl.loop(0, 4)
        def _(d):
            to = chunk * 4 + d

            @pl.when(to != me)
            def _():
                mode_send(to).start()

            @pl.when(to == me)
            def _():
                mode_keep().start()

    @pl.loop(0, 8)
    def _(s):
        @pl.loop(0, 4)
        def _(j):
            source = s + 8 * j

            @pl.when(source != me)
            def _():
                mode_recv(source).wait_recv()

            @pl.when(source == me)
            def _():
                mode_keep().wait()

        re = [recv_ref[s + 8 * j, 0] for j in range(4)]
        im = [recv_ref[s + 8 * j, 1] for j in range(4)]
        for r, pair in enumerate(residues(re, im)):
            for part in range(2):
                high, low = split(pair[part])
                rows = pl.ds(pl.multiple_of(part * 256 + s * 32, 32), 32)
                pair_ref[r, rows, 0:128] = high
                pair_ref[r, rows, 128:256] = low

    z_copy.wait()

    @pl.loop(0, 4)
    def _(r):
        p = dot(z_ref[r], pair_ref[r])
        field_ref[r] = (p[:256, :128] + p[:256, 128:]) + (p[256:, :128] + p[256:, 128:])

    @pl.loop(0, 32)
    def _(step):
        rows = pl.ds(pl.multiple_of(step * 8, 8), 8)
        parts = [field_ref[r, rows, :] for r in range(4)]
        pack_ref[0, rows, :] = shuffle(parts, 3)
        pack_ref[1, rows, :] = shuffle(parts, 0)

    halos = [
        pltpu.make_async_remote_copy(
            src_ref=pack_ref.at[side], dst_ref=halo_ref.at[side], send_sem=halo_send.at[side],
            recv_sem=halo_recv.at[side], device_id={"plane": to}, device_id_type=MESH,
        )
        for side, to in ((0, next_plane), (1, last_plane))
    ]
    for halo in halos:
        halo.start()

    def own_rows(slab):
        return field_ref.at[:, pl.ds(pl.multiple_of(slab * 8, 8), 8), :]

    def slab_send_copy(to):
        return pltpu.make_async_remote_copy(
            src_ref=own_rows(to), dst_ref=slab_ref.at[me], send_sem=slab_send.at[to], recv_sem=slab_recv.at[me],
            device_id={"depth": to}, device_id_type=MESH,
        )

    def slab_recv_copy(source):
        return pltpu.make_async_remote_copy(
            src_ref=own_rows(source), dst_ref=slab_ref.at[source], send_sem=slab_send.at[source],
            recv_sem=slab_recv.at[source], device_id={"depth": source}, device_id_type=MESH,
        )

    slab_keep = pltpu.make_async_copy(own_rows(me), slab_ref.at[me], slab_recv.at[me])
    slab_keep.start()

    @pl.loop(1, 32)
    def _(step):
        slab_send_copy(lax.rem(me + step, 32)).start()

    coeffs = coefficients(coeff_ref, index_ref)
    for halo in halos:
        halo.wait_recv()

    @pl.loop(0, 32)
    def _(step):
        rows = pl.ds(pl.multiple_of(step * 8, 8), 8)
        for r in range(4):
            light_ref[r, rows, :] = lighting(field_ref[r, rows, :], halo_ref[0, rows, :], halo_ref[1, rows, :], r)

    def body(step, state):
        rows = pl.ds(pl.multiple_of(step * 8, 8), 8)
        for k in range(8):
            for r in range(4):
                s = jnp.broadcast_to(field_ref[r, rows, :][k : k + 1, :], (8, 128))
                light = jnp.broadcast_to(light_ref[r, rows, :][k : k + 1, :], (8, 128))
                state = render_step(coeffs, s, light, state)
        return state

    zero = jnp.zeros((8, 128), f32)
    c0, c1, c2, _, depth_sum = lax.fori_loop(0, 32, body, (zero, zero, zero, zero + 1.0, zero))
    image_out[0] = c0
    image_out[1] = c1
    image_out[2] = c2
    image_out[3] = jnp.exp(depth_sum * -tau_scale)

    slab_keep.wait()

    @pl.loop(1, 32)
    def _(step):
        slab_recv_copy(lax.rem(me + step, 32)).wait_recv()

    @pl.loop(0, 8)
    def _(g):
        for r in range(4):
            parts = [slab_ref[g * 4 + d, r] for d in range(4)]
            for y in range(4):
                field_out[pl.ds(r * 32 + g * 4 + y, 8, stride=128), :] = shuffle(parts, y)

    @pl.loop(1, 32)
    def _(step):
        to = lax.rem(me + step, 32)
        mode_send(to).wait_send()
        slab_send_copy(to).wait_send()

    for halo in halos:
        halo.wait_send()


def body(x_tab, z_tab, spectrum, transfer_coeffs, transfer_index):
    smem = pl.BlockSpec(memory_space=pltpu.SMEM)
    vmem = pl.BlockSpec(memory_space=pltpu.VMEM)
    hbm = pl.BlockSpec(memory_space=pl.ANY)
    sem = pltpu.SemaphoreType.DMA
    field, image = pl.pallas_call(
        kernel,
        out_shape=[jax.ShapeDtypeStruct((1024, 128), f32), jax.ShapeDtypeStruct((4, 8, 128), f32)],
        in_specs=[smem, smem, vmem, hbm, hbm],
        out_specs=[vmem, vmem],
        scratch_shapes=[
            pltpu.VMEM((8, 2, NX, 256), bf16),
            pltpu.VMEM((4, 512, 512), bf16),
            pltpu.VMEM((2, 128, 128), f32),
            pltpu.VMEM((32, 2, 32, 128), f32),
            pltpu.VMEM((32, 2, 32, 128), f32),
            pltpu.VMEM((4, 512, 256), bf16),
            pltpu.VMEM((4, 256, 128), f32),
            pltpu.VMEM((4, 256, 128), f32),
            pltpu.VMEM((2, 256, 128), f32),
            pltpu.VMEM((2, 256, 128), f32),
            pltpu.VMEM((32, 4, 8, 128), f32),
            sem((8,)), sem, sem((32,)), sem((32,)), sem((2,)), sem((2,)), sem((32,)), sem((32,)),
        ],
        compiler_params=pltpu.CompilerParams(
            collective_id=0, has_side_effects=True, vmem_limit_bytes=40 * 2**20
        ),
    )(transfer_coeffs.reshape(8, 16), transfer_index, spectrum.reshape(256, NX), x_tab, z_tab)
    scalar_field = field.reshape(32, 8, 4, 128).transpose(0, 2, 1, 3).reshape(32, 4, NX)
    rendered = jnp.transpose(image.reshape(4, 8, 4, 32), (1, 0, 2, 3))
    return scalar_field, rendered


def solution(mesh):
    x_tab, z_tab = x_table(), z_table()
    mapped = jax.shard_map(
        body,
        mesh=mesh,
        in_specs=(P(), P(), P(None, "depth", "plane", None), P(), P()),
        out_specs=(P("depth", "plane", None), P(None, None, "plane", "depth")),
        check_vma=False,
    )

    def run(spectrum, transfer_coeffs, transfer_index):
        return mapped(x_tab, z_tab, spectrum, transfer_coeffs, transfer_index)

    return run
```

```python
import math

import jax
import jax.numpy as jnp
import ml_dtypes
import numpy as np
from jax import lax
from jax.experimental import pallas as pl
from jax.experimental.pallas import tpu as pltpu
from jax.sharding import PartitionSpec as P

NX = 1024
NZ = 1024
density = 2.0
shade_gain = 0.4
tau_scale = density / NZ
LN2 = math.log(2.0)
f32 = jnp.float32
bf16 = jnp.bfloat16
MESH = pl.DeviceIdType.MESH


def split_table(values):
    high = values.astype(ml_dtypes.bfloat16)
    low = (values - high.astype(np.float64)).astype(ml_dtypes.bfloat16)
    return np.stack([high, low])


def x_table():
    index = np.arange(NX)
    angles = (index[:, None] * index[None, :] % NX) * (2.0 * np.pi / NX)
    tables = [split_table(t / math.sqrt(NX)).reshape(2, NX, 8, 128) for t in (np.cos(angles), np.sin(angles))]
    return np.ascontiguousarray(np.concatenate(tables, axis=3).transpose(2, 0, 1, 3))


def z_table():
    q0 = np.arange(256)
    m = np.arange(256)
    tables = []
    for r in range(4):
        angles = (q0[None, :] * (4 * m[:, None] + r) % NZ) * (2.0 * np.pi / NZ)
        table = np.concatenate([np.cos(angles), -np.sin(angles)], axis=1) / math.sqrt(NZ)
        tables.append(split_table(table).reshape(512, 512))
    return np.stack(tables)


def split(value):
    high = value.astype(bf16)
    return high, (value - high.astype(f32)).astype(bf16)


def dot(a, b):
    return jnp.dot(a, b, preferred_element_type=f32)


def residues(re, im):
    a, b = re[0] + re[2], im[0] + im[2]
    c, d = re[0] - re[2], im[0] - im[2]
    e, f = re[1] + re[3], im[1] + im[3]
    g, h = re[1] - re[3], im[1] - im[3]
    return [(a + e, b + f), (c - h, d + g), (a - e, b - f), (c + h, d - g)]


def lighting(field, before, after, r):
    lane = lax.broadcasted_iota(jnp.int32, field.shape, 1)
    up = pltpu.roll(field, 96, 1)
    down = pltpu.roll(field, 32, 1)
    after = pltpu.roll(after, (96 - 32 * r) % 128, 1) if r != 3 else after
    before = pltpu.roll(before, (-32 * r) % 128, 1) if r else before
    up = jnp.where(lane >= 96, after, up)
    down = jnp.where(lane < 32, before, down)
    return 1.0 + shade_gain * jnp.tanh(0.5 * (up - down))


def coefficients(coeff_ref, index_ref):
    row = lax.broadcasted_iota(jnp.int32, (8, 128), 0)
    result = []
    for channel in range(4):
        for n in range(4):
            value = jnp.zeros((8, 128), f32)
            for image in range(8):
                value = jnp.where(row == image, coeff_ref[channel, n, index_ref[image]], value)
            result.append(value)
    return result


def encode(parts):
    peak = jnp.maximum(jnp.abs(parts[0]), jnp.abs(parts[1]))
    peak = jnp.maximum(jnp.max(peak, axis=0, keepdims=True), 1e-30)
    level = jnp.floor(jnp.log(peak) * (256.0 / LN2)) + 2.0
    level = jnp.broadcast_to(level, (16, 128))
    scale = jnp.exp2(level[:8] * (-1.0 / 256.0)) * 32766.0
    scale = jnp.concatenate([scale] * 4)
    codes = [jnp.round(part * scale).astype(jnp.int32).astype(jnp.int16) for part in parts]
    return codes, level.astype(jnp.int32).astype(jnp.int16)


def decode(codes, level):
    step = jnp.exp2(level.astype(jnp.int32).astype(f32)[:8] * (1.0 / 256.0)) * (1.0 / 32766.0)
    step = jnp.concatenate([step] * 4)
    return [code.astype(jnp.int32).astype(f32) * step for code in codes]


def softplus(coeffs, s):
    p = ((coeffs[3] * s + coeffs[2]) * s + coeffs[1]) * s + coeffs[0]
    return jnp.maximum(p, jnp.log(1.0 + jnp.exp(jnp.minimum(p, 80.0))))


def opacity(depth):
    k1, k2, k3 = tau_scale, tau_scale**2 / 2, tau_scale**3 / 6
    small = depth * (k1 - depth * (k2 - depth * k3))
    large = 1.0 - jnp.exp(depth * -tau_scale)
    return jnp.where(depth < 16.0, small, large)


def render_step(coeffs, s, light, state):
    c0, c1, c2, through, depth_sum = state
    depth = softplus(coeffs[12:16], s)
    weight = through * opacity(depth)
    through = through - weight
    weight = weight * light
    c0 = c0 + weight * softplus(coeffs[0:4], s)
    c1 = c1 + weight * softplus(coeffs[4:8], s)
    c2 = c2 + weight * softplus(coeffs[8:12], s)
    return c0, c1, c2, through, depth_sum + depth


def shuffle(parts, place):
    group = lax.broadcasted_iota(jnp.int32, parts[0].shape, 1) // 32
    result = None
    for g in range(4):
        shift = (32 * (g - place)) % 128
        moved = pltpu.roll(parts[g], shift, 1) if shift else parts[g]
        result = moved if result is None else jnp.where(group == g, moved, result)
    return result


def kernel(
    coeff_ref, index_ref, spectrum_ref, x_hbm, z_hbm,
    field_out, image_out,
    row_ref, x_ref, z_ref, mode_ref, send_ref, recv_ref, pair_ref, field_ref, light_ref, pack_ref, halo_ref, slab_ref,
    x_sem, z_sem, send_sem, recv_sem, halo_send, halo_recv, slab_send, slab_recv,
):
    me = lax.axis_index("depth")
    plane = lax.axis_index("plane")
    planes = lax.axis_size("plane")
    next_plane = lax.rem(plane + 1, planes)
    last_plane = lax.rem(plane + planes - 1, planes)

    def chunk_of(step):
        return lax.rem(me // 4 + step, 8)

    def x_copy(step):
        chunk = chunk_of(step)
        return pltpu.make_async_copy(x_hbm.at[chunk], x_ref.at[chunk], x_sem.at[step])

    z_copy = pltpu.make_async_copy(z_hbm, z_ref, z_sem)

    @pl.loop(0, 8)
    def _(step):
        x_copy(step).start()

    z_copy.start()

    barrier = pltpu.get_barrier_semaphore()

    @pl.loop(1, 32)
    def _(step):
        pl.semaphore_signal(barrier, inc=1, device_id={"depth": lax.rem(me + step, 32)}, device_id_type=MESH)

    pl.semaphore_signal(barrier, inc=1, device_id={"plane": next_plane}, device_id_type=MESH)
    pl.semaphore_signal(barrier, inc=1, device_id={"plane": last_plane}, device_id_type=MESH)

    def mode_send(to):
        return pltpu.make_async_remote_copy(
            src_ref=send_ref.at[to], dst_ref=recv_ref.at[me], send_sem=send_sem.at[to], recv_sem=recv_sem.at[me],
            device_id={"depth": to}, device_id_type=MESH,
        )

    def mode_recv(source):
        return pltpu.make_async_remote_copy(
            src_ref=send_ref.at[source], dst_ref=recv_ref.at[source], send_sem=send_sem.at[source],
            recv_sem=recv_sem.at[source], device_id={"depth": source}, device_id_type=MESH,
        )

    def mode_keep():
        return pltpu.make_async_copy(send_ref.at[me], recv_ref.at[me], recv_sem.at[me])

    row_ref[...] = spectrum_ref[...].reshape(256, NX)

    @pl.loop(0, 8)
    def _(step):
        chunk = chunk_of(step)
        x_copy(step).wait()
        modes = row_ref[...]
        waves = dot(modes, x_ref[chunk, 0]) + dot(modes, x_ref[chunk, 1])
        mode_ref[0] = waves[:128, :128] - waves[128:, 128:]
        mode_ref[1] = waves[:128, 128:] + waves[128:, :128]
        parts = [[] for _ in range(4)]
        for part in range(2):
            rows = [mode_ref[part, pl.ds(y, 32, stride=4), :] for y in range(4)]
            for d in range(4):
                parts[d].append(shuffle(rows, d))
        for d in range(4):
            codes, level = encode(parts[d])
            send_ref[chunk * 4 + d, 0:32] = codes[0]
            send_ref[chunk * 4 + d, 32:64] = codes[1]
            send_ref[chunk * 4 + d, 64:80] = level

        @pl.when(step == 0)
        def _():
            pl.semaphore_wait(barrier, 33)

        @pl.loop(0, 4)
        def _(d):
            to = chunk * 4 + d

            @pl.when(to != me)
            def _():
                mode_send(to).start()

            @pl.when(to == me)
            def _():
                mode_keep().start()

    @pl.loop(0, 8)
    def _(s):
        @pl.loop(0, 4)
        def _(j):
            source = s + 8 * j

            @pl.when(source != me)
            def _():
                mode_recv(source).wait_recv()

            @pl.when(source == me)
            def _():
                mode_keep().wait()

        re, im = [], []
        for j in range(4):
            got = recv_ref.at[s + 8 * j]
            real, imag = decode([got[0:32], got[32:64]], got[64:80])
            re.append(real)
            im.append(imag)
        for r, pair in enumerate(residues(re, im)):
            for part in range(2):
                high, low = split(pair[part])
                rows = pl.ds(pl.multiple_of(part * 256 + s * 32, 32), 32)
                pair_ref[r, rows, 0:128] = high
                pair_ref[r, rows, 128:256] = low

    z_copy.wait()

    @pl.loop(0, 4)
    def _(r):
        p = dot(z_ref[r], pair_ref[r])
        field_ref[r] = (p[:256, :128] + p[:256, 128:]) + (p[256:, :128] + p[256:, 128:])

    @pl.loop(0, 32)
    def _(step):
        rows = pl.ds(pl.multiple_of(step * 8, 8), 8)
        parts = [field_ref[r, rows, :] for r in range(4)]
        pack_ref[0, rows, :] = shuffle(parts, 3)
        pack_ref[1, rows, :] = shuffle(parts, 0)

    halos = [
        pltpu.make_async_remote_copy(
            src_ref=pack_ref.at[side], dst_ref=halo_ref.at[side], send_sem=halo_send.at[side],
            recv_sem=halo_recv.at[side], device_id={"plane": to}, device_id_type=MESH,
        )
        for side, to in ((0, next_plane), (1, last_plane))
    ]
    for halo in halos:
        halo.start()

    def own_rows(slab):
        return field_ref.at[:, pl.ds(pl.multiple_of(slab * 8, 8), 8), :]

    def slab_send_copy(to):
        return pltpu.make_async_remote_copy(
            src_ref=own_rows(to), dst_ref=slab_ref.at[me], send_sem=slab_send.at[to], recv_sem=slab_recv.at[me],
            device_id={"depth": to}, device_id_type=MESH,
        )

    def slab_recv_copy(source):
        return pltpu.make_async_remote_copy(
            src_ref=own_rows(source), dst_ref=slab_ref.at[source], send_sem=slab_send.at[source],
            recv_sem=slab_recv.at[source], device_id={"depth": source}, device_id_type=MESH,
        )

    slab_keep = pltpu.make_async_copy(own_rows(me), slab_ref.at[me], slab_recv.at[me])

    coeffs = coefficients(coeff_ref, index_ref)
    for halo in halos:
        halo.wait_recv()

    slab_keep.start()

    @pl.loop(0, 32)
    def _(step):
        @pl.when(step > 0)
        def _():
            slab_send_copy(lax.rem(me + step, 32)).start()

        rows = pl.ds(pl.multiple_of(step * 8, 8), 8)
        for r in range(4):
            light_ref[r, rows, :] = lighting(field_ref[r, rows, :], halo_ref[0, rows, :], halo_ref[1, rows, :], r)

    def body(step, state):
        rows = pl.ds(pl.multiple_of(step * 8, 8), 8)
        for k in range(8):
            for r in range(4):
                s = jnp.broadcast_to(field_ref[r, rows, :][k : k + 1, :], (8, 128))
                light = jnp.broadcast_to(light_ref[r, rows, :][k : k + 1, :], (8, 128))
                state = render_step(coeffs, s, light, state)
        return state

    zero = jnp.zeros((8, 128), f32)
    c0, c1, c2, _, depth_sum = lax.fori_loop(0, 32, body, (zero, zero, zero, zero + 1.0, zero))
    for channel, image in enumerate((c0, c1, c2, jnp.exp(depth_sum * -tau_scale))):
        for y in range(4):
            moved = pltpu.roll(image, 128 - 32 * y, 1) if y else image
            image_out[pl.ds(channel * 4 + y, 8, stride=16), :] = moved

    slab_keep.wait()

    @pl.loop(1, 32)
    def _(step):
        slab_recv_copy(lax.rem(me + step, 32)).wait_recv()

    @pl.loop(0, 8)
    def _(g):
        for r in range(4):
            parts = [slab_ref[g * 4 + d, r] for d in range(4)]
            for y in range(4):
                field_out[pl.ds(r * 32 + g * 4 + y, 8, stride=128), :] = shuffle(parts, y)

    @pl.loop(1, 32)
    def _(step):
        to = lax.rem(me + step, 32)
        mode_send(to).wait_send()
        slab_send_copy(to).wait_send()

    for halo in halos:
        halo.wait_send()


def body(x_tab, z_tab, spectrum, transfer_coeffs, transfer_index):
    smem = pl.BlockSpec(memory_space=pltpu.SMEM)
    vmem = pl.BlockSpec(memory_space=pltpu.VMEM)
    hbm = pl.BlockSpec(memory_space=pl.ANY)
    sem = pltpu.SemaphoreType.DMA
    field, image = pl.pallas_call(
        kernel,
        out_shape=[jax.ShapeDtypeStruct((1024, 128), f32), jax.ShapeDtypeStruct((128, 128), f32)],
        in_specs=[smem, smem, vmem, hbm, hbm],
        out_specs=[vmem, vmem],
        scratch_shapes=[
            pltpu.VMEM((256, NX), bf16),
            pltpu.VMEM((8, 2, NX, 256), bf16),
            pltpu.VMEM((4, 512, 512), bf16),
            pltpu.VMEM((2, 128, 128), f32),
            pltpu.VMEM((32, 80, 128), jnp.int16),
            pltpu.VMEM((32, 80, 128), jnp.int16),
            pltpu.VMEM((4, 512, 256), bf16),
            pltpu.VMEM((4, 256, 128), f32),
            pltpu.VMEM((4, 256, 128), f32),
            pltpu.VMEM((2, 256, 128), f32),
            pltpu.VMEM((2, 256, 128), f32),
            pltpu.VMEM((32, 4, 8, 128), f32),
            sem((8,)), sem, sem((32,)), sem((32,)), sem((2,)), sem((2,)), sem((32,)), sem((32,)),
        ],
        compiler_params=pltpu.CompilerParams(
            collective_id=0, has_side_effects=True, vmem_limit_bytes=60 * 2**20
        ),
    )(transfer_coeffs.transpose(1, 2, 0), transfer_index, spectrum, x_tab, z_tab)
    scalar_field = field.reshape(32, 8, 4, 128).transpose(0, 2, 1, 3).reshape(32, 4, NX)
    rendered = image[:, :32].reshape(8, 4, 4, 32)
    return scalar_field, rendered


def solution(mesh):
    x_tab, z_tab = x_table(), z_table()
    mapped = jax.shard_map(
        body,
        mesh=mesh,
        in_specs=(P(), P(), P(None, "depth", "plane", None), P(), P()),
        out_specs=(P("depth", "plane", None), P(None, None, "plane", "depth")),
        check_vma=False,
    )

    def run(spectrum, transfer_coeffs, transfer_index):
        return mapped(x_tab, z_tab, spectrum, transfer_coeffs, transfer_index)

    return run
```

```python
import math

import jax
import jax.numpy as jnp
import ml_dtypes
import numpy as np
from jax import lax
from jax.experimental import pallas as pl
from jax.experimental.pallas import tpu as pltpu
from jax.sharding import PartitionSpec as P

NX = 1024
NZ = 1024
density = 2.0
shade_gain = 0.4
tau_scale = density / NZ
f32 = jnp.float32
bf16 = jnp.bfloat16
MESH = pl.DeviceIdType.MESH


def split_table(values):
    high = values.astype(ml_dtypes.bfloat16)
    low = (values - high.astype(np.float64)).astype(ml_dtypes.bfloat16)
    return np.stack([high, low])


def x_table():
    k = 4 * np.arange(256)[None, :, None] + np.arange(4)[:, None, None]
    angles = (k * np.arange(256)[None, None, :] % NX) * (2.0 * np.pi / NX)
    tables = [split_table(t / math.sqrt(NX)).reshape(2, 4, 256, 2, 128) for t in (np.cos(angles), np.sin(angles))]
    return np.ascontiguousarray(np.concatenate(tables, axis=4).transpose(3, 0, 1, 2, 4))


def z_table():
    q0 = np.arange(256)
    m = np.arange(256)
    tables = []
    for r in range(4):
        angles = (q0[None, :] * (4 * m[:, None] + r) % NZ) * (2.0 * np.pi / NZ)
        table = np.concatenate([np.cos(angles), -np.sin(angles)], axis=1) / math.sqrt(NZ)
        tables.append(split_table(table).reshape(512, 512))
    return np.stack(tables)


def split(value):
    high = value.astype(bf16)
    return high, (value - high.astype(f32)).astype(bf16)


def dot(a, b):
    return jnp.dot(a, b, preferred_element_type=f32)


def residues(re, im):
    a, b = re[0] + re[2], im[0] + im[2]
    c, d = re[0] - re[2], im[0] - im[2]
    e, f = re[1] + re[3], im[1] + im[3]
    g, h = re[1] - re[3], im[1] - im[3]
    return [(a + e, b + f), (c - h, d + g), (a - e, b - f), (c + h, d - g)]


def lighting(field, before, after, r):
    lane = lax.broadcasted_iota(jnp.int32, field.shape, 1)
    up = pltpu.roll(field, 96, 1)
    down = pltpu.roll(field, 32, 1)
    after = pltpu.roll(after, (96 - 32 * r) % 128, 1) if r != 3 else after
    before = pltpu.roll(before, (-32 * r) % 128, 1) if r else before
    up = jnp.where(lane >= 96, after, up)
    down = jnp.where(lane < 32, before, down)
    return 1.0 + shade_gain * jnp.tanh(0.5 * (up - down))


def coefficients(coeff_ref, index_ref):
    row = lax.broadcasted_iota(jnp.int32, (8, 128), 0)
    result = []
    for channel in range(4):
        for n in range(4):
            value = jnp.zeros((8, 128), f32)
            for image in range(8):
                value = jnp.where(row == image, coeff_ref[channel, n, index_ref[image]], value)
            result.append(value)
    return result


def encode(parts):
    peak = jnp.maximum(jnp.abs(parts[0]), jnp.abs(parts[1]))
    peak = jnp.maximum(jnp.max(peak, axis=0, keepdims=True), 1e-30)
    codes = [jnp.round(part * (32766.0 / peak)).astype(jnp.int32).astype(jnp.int16) for part in parts]
    return codes, peak * (1.0 / 32766.0)


def decode(codes, step):
    return [code.astype(jnp.int32).astype(f32) * step for code in codes]


def gather_classes(rows_ref, class_ref):
    source = lax.broadcasted_iota(jnp.int32, (256, 256), 0)
    target = lax.broadcasted_iota(jnp.int32, (256, 256), 1)
    move = jnp.where(source == 4 * (target % 64) + target // 64, 1.0, 0.0).astype(bf16)
    low_half = lax.broadcasted_iota(jnp.int32, (256, 128), 1) < 64
    for half in range(2):
        p = [dot(rows_ref[:, 512 * half + 256 * t : 512 * half + 256 * (t + 1)], move) for t in range(2)]
        for j in range(4):
            a, b = (q[:, 128 * (j // 2) : 128 * (j // 2 + 1)] for q in p)
            if j % 2 == 0:
                value = jnp.where(low_half, a, pltpu.roll(b, 64, 1))
            else:
                value = jnp.where(low_half, pltpu.roll(a, 64, 1), b)
            class_ref[j, :, 128 * half : 128 * (half + 1)] = value.astype(bf16)


def softplus(coeffs, s):
    p = ((coeffs[3] * s + coeffs[2]) * s + coeffs[1]) * s + coeffs[0]
    return jnp.maximum(p, jnp.log(1.0 + jnp.exp(jnp.minimum(p, 80.0))))


def opacity(depth):
    k1, k2, k3 = tau_scale, tau_scale**2 / 2, tau_scale**3 / 6
    small = depth * (k1 - depth * (k2 - depth * k3))
    large = 1.0 - jnp.exp(depth * -tau_scale)
    return jnp.where(depth < 16.0, small, large)


def render_step(coeffs, s, light, state):
    c0, c1, c2, through, depth_sum = state
    depth = softplus(coeffs[12:16], s)
    weight = through * opacity(depth)
    through = through - weight
    weight = weight * light
    c0 = c0 + weight * softplus(coeffs[0:4], s)
    c1 = c1 + weight * softplus(coeffs[4:8], s)
    c2 = c2 + weight * softplus(coeffs[8:12], s)
    return c0, c1, c2, through, depth_sum + depth


def shuffle(parts, place):
    group = lax.broadcasted_iota(jnp.int32, parts[0].shape, 1) // 32
    result = None
    for g in range(4):
        shift = (32 * (g - place)) % 128
        moved = pltpu.roll(parts[g], shift, 1) if shift else parts[g]
        result = moved if result is None else jnp.where(group == g, moved, result)
    return result


def kernel(
    coeff_ref, index_ref, spectrum_ref, x_hbm, z_hbm,
    field_out, image_out,
    row_ref, class_ref, x_ref, z_ref, wave_ref, mode_ref, send_ref, recv_ref, step_out, step_in, pair_ref, value_ref, glow_ref, field_ref, light_ref, pack_ref, halo_ref, slab_ref,
    x_sem, z_sem, send_sem, recv_sem, halo_send, halo_recv, slab_send, slab_recv,
):
    me = lax.axis_index("depth")
    plane = lax.axis_index("plane")
    planes = lax.axis_size("plane")
    next_plane = lax.rem(plane + 1, planes)
    last_plane = lax.rem(plane + planes - 1, planes)

    def half_of(step):
        return lax.rem(me // 4 + step, 2)

    def x_copy(step):
        half = half_of(step)
        return pltpu.make_async_copy(x_hbm.at[half], x_ref.at[half], x_sem.at[step])

    z_copy = pltpu.make_async_copy(z_hbm, z_ref, z_sem)

    for step in range(2):
        x_copy(step).start()

    z_copy.start()

    barrier = pltpu.get_barrier_semaphore()

    @pl.loop(1, 32)
    def _(step):
        pl.semaphore_signal(barrier, inc=1, device_id={"depth": lax.rem(me + step, 32)}, device_id_type=MESH)

    pl.semaphore_signal(barrier, inc=1, device_id={"plane": next_plane}, device_id_type=MESH)
    pl.semaphore_signal(barrier, inc=1, device_id={"plane": last_plane}, device_id_type=MESH)

    def mode_sends(to):
        return [
            pltpu.make_async_remote_copy(
                src_ref=out_ref.at[to], dst_ref=in_ref.at[me], send_sem=send_sem.at[k, to], recv_sem=recv_sem.at[k, me],
                device_id={"depth": to}, device_id_type=MESH,
            )
            for k, (out_ref, in_ref) in enumerate(((send_ref, recv_ref), (step_out, step_in)))
        ]

    def mode_recvs(source):
        return [
            pltpu.make_async_remote_copy(
                src_ref=out_ref.at[source], dst_ref=in_ref.at[source], send_sem=send_sem.at[k, source],
                recv_sem=recv_sem.at[k, source], device_id={"depth": source}, device_id_type=MESH,
            )
            for k, (out_ref, in_ref) in enumerate(((send_ref, recv_ref), (step_out, step_in)))
        ]

    def mode_keeps():
        return [
            pltpu.make_async_copy(out_ref.at[me], in_ref.at[me], recv_sem.at[k, me])
            for k, (out_ref, in_ref) in enumerate(((send_ref, recv_ref), (step_out, step_in)))
        ]

    row_ref[...] = spectrum_ref[...].reshape(256, NX)
    gather_classes(row_ref, class_ref)

    @pl.loop(0, 2)
    def _(step):
        half = half_of(step)
        x_copy(step).wait()
        for j in range(4):
            waves = dot(class_ref[j], x_ref[half, 0, j]) + dot(class_ref[j], x_ref[half, 1, j])
            wave_ref[j, 0] = waves[:128, :128] - waves[128:, 128:]
            wave_ref[j, 1] = waves[:128, 128:] + waves[128:, :128]
        for k in range(4):
            rows = slice(32 * k, 32 * k + 32)
            re = [wave_ref[j, 0, rows] for j in range(4)]
            im = [wave_ref[j, 1, rows] for j in range(4)]
            for i, pair in enumerate(residues(re, im)):
                mode_ref[i, 0, rows] = pair[0]
                mode_ref[i, 1, rows] = pair[1]

        @pl.when(step == 0)
        def _():
            pl.semaphore_wait(barrier, 33)

        @pl.loop(0, 4)
        def _(turn):
            i = lax.rem(me // 8 + turn + turn // 2 - 2 * (turn // 3), 4)
            first = 8 * i + 4 * half
            parts = [[] for _ in range(4)]
            for part in range(2):
                rows = [mode_ref[i, part, pl.ds(y, 32, stride=4), :] for y in range(4)]
                for d in range(4):
                    parts[d].append(shuffle(rows, d))
            for d in range(4):
                codes, size = encode(parts[d])
                send_ref[first + d, 0:32] = codes[0]
                send_ref[first + d, 32:64] = codes[1]
                step_out[first + d] = size

            @pl.loop(0, 4)
            def _(d):
                to = first + d

                @pl.when(to != me)
                def _():
                    for copy in mode_sends(to):
                        copy.start()

                @pl.when(to == me)
                def _():
                    for copy in mode_keeps():
                        copy.start()

    coeffs = coefficients(coeff_ref, index_ref)
    for n, value in enumerate(coeffs):
        value_ref[n] = value

    @pl.loop(0, 8)
    def _(s):
        @pl.loop(0, 4)
        def _(j):
            source = s + 8 * j

            @pl.when(source != me)
            def _():
                for copy in mode_recvs(source):
                    copy.wait_recv()

            @pl.when(source == me)
            def _():
                for copy in mode_keeps():
                    copy.wait()

        re, im = [], []
        for j in range(4):
            got = recv_ref.at[s + 8 * j]
            real, imag = decode([got[0:32], got[32:64]], step_in[s + 8 * j])
            re.append(real)
            im.append(imag)
        for r, pair in enumerate(residues(re, im)):
            for part in range(2):
                high, low = split(pair[part])
                rows = pl.ds(pl.multiple_of(part * 256 + s * 32, 32), 32)
                pair_ref[r, rows, 0:128] = high
                pair_ref[r, rows, 128:256] = low

    z_copy.wait()

    @pl.loop(0, 4)
    def _(r):
        p = dot(z_ref[r], pair_ref[r])
        field_ref[r] = (p[:256, :128] + p[:256, 128:]) + (p[256:, :128] + p[256:, 128:])

    @pl.loop(0, 4)
    def _(step):
        rows = pl.ds(pl.multiple_of(step * 64, 64), 64)
        parts = [field_ref[r, rows, :] for r in range(4)]
        pack_ref[0, rows, :] = shuffle(parts, 3)
        pack_ref[1, rows, :] = shuffle(parts, 0)

    halos = [
        pltpu.make_async_remote_copy(
            src_ref=pack_ref.at[side], dst_ref=halo_ref.at[side], send_sem=halo_send.at[side],
            recv_sem=halo_recv.at[side], device_id={"plane": to}, device_id_type=MESH,
        )
        for side, to in ((0, next_plane), (1, last_plane))
    ]
    for halo in halos:
        halo.start()

    def own_rows(slab):
        return field_ref.at[:, pl.ds(pl.multiple_of(slab * 8, 8), 8), :]

    def slab_send_copy(to):
        return pltpu.make_async_remote_copy(
            src_ref=own_rows(to), dst_ref=slab_ref.at[me], send_sem=slab_send.at[to], recv_sem=slab_recv.at[me],
            device_id={"depth": to}, device_id_type=MESH,
        )

    def slab_recv_copy(source):
        return pltpu.make_async_remote_copy(
            src_ref=own_rows(source), dst_ref=slab_ref.at[source], send_sem=slab_send.at[source],
            recv_sem=slab_recv.at[source], device_id={"depth": source}, device_id_type=MESH,
        )

    slab_keep = pltpu.make_async_copy(own_rows(me), slab_ref.at[me], slab_recv.at[me])

    slab_keep.start()
    coeffs = [value_ref[n] for n in range(16)]

    def cell_row(ref, step, r, k):
        rows = pl.ds(pl.multiple_of(step * 8, 8), 8)
        return jnp.broadcast_to(ref[r, rows, :][k : k + 1, :], (8, 128))

    def front(step, state):
        @pl.loop(0, 2)
        def _(n):
            @pl.when(2 * step + n > 0)
            def _():
                slab_send_copy(lax.rem(me + 2 * step + n, 32)).start()

        through, depth_sum = state
        for k in range(8):
            for r in range(4):
                s = cell_row(field_ref, step, r, k)
                depth = softplus(coeffs[12:16], s)
                weight = through * opacity(depth)
                through = through - weight
                depth_sum = depth_sum + depth
                for j in range(3):
                    glow_ref[step, 4 * k + r, j] = weight * softplus(coeffs[4 * j : 4 * j + 4], s)
        return through, depth_sum

    zero = jnp.zeros((8, 128), f32)
    through, depth_sum = lax.fori_loop(0, 16, front, (zero + 1.0, zero))

    for halo in halos:
        halo.wait_recv()

    @pl.loop(0, 8)
    def _(step):
        rows = pl.ds(pl.multiple_of(step * 32, 32), 32)
        for r in range(4):
            light_ref[r, rows, :] = lighting(field_ref[r, rows, :], halo_ref[0, rows, :], halo_ref[1, rows, :], r)

    def lit(step, colors):
        colors = list(colors)
        for k in range(8):
            for r in range(4):
                light = cell_row(light_ref, step, r, k)
                for j in range(3):
                    colors[j] = colors[j] + light * glow_ref[step, 4 * k + r, j]
        return tuple(colors)

    colors = lax.fori_loop(0, 16, lit, (zero, zero, zero))

    def body(step, state):
        for k in range(8):
            for r in range(4):
                s = cell_row(field_ref, step, r, k)
                state = render_step(coeffs, s, cell_row(light_ref, step, r, k), state)
        return state

    c0, c1, c2, _, depth_sum = lax.fori_loop(16, 32, body, (*colors, through, depth_sum))
    for channel, image in enumerate((c0, c1, c2, jnp.exp(depth_sum * -tau_scale))):
        for y in range(4):
            moved = pltpu.roll(image, 128 - 32 * y, 1) if y else image
            image_out[pl.ds(channel * 4 + y, 8, stride=16), :] = moved

    slab_keep.wait()

    @pl.loop(1, 32)
    def _(step):
        slab_recv_copy(lax.rem(me + step, 32)).wait_recv()

    @pl.loop(0, 8)
    def _(g):
        for r in range(4):
            parts = [slab_ref[g * 4 + d, r] for d in range(4)]
            for y in range(4):
                field_out[pl.ds(r * 32 + g * 4 + y, 8, stride=128), :] = shuffle(parts, y)

    @pl.loop(1, 32)
    def _(step):
        to = lax.rem(me + step, 32)
        for copy in mode_sends(to):
            copy.wait_send()
        slab_send_copy(to).wait_send()

    for halo in halos:
        halo.wait_send()


def body(x_tab, z_tab, spectrum, transfer_coeffs, transfer_index):
    smem = pl.BlockSpec(memory_space=pltpu.SMEM)
    vmem = pl.BlockSpec(memory_space=pltpu.VMEM)
    hbm = pl.BlockSpec(memory_space=pl.ANY)
    sem = pltpu.SemaphoreType.DMA
    field, image = pl.pallas_call(
        kernel,
        out_shape=[jax.ShapeDtypeStruct((1024, 128), f32), jax.ShapeDtypeStruct((128, 128), f32)],
        in_specs=[smem, smem, vmem, hbm, hbm],
        out_specs=[vmem, vmem],
        scratch_shapes=[
            pltpu.VMEM((256, NX), bf16),
            pltpu.VMEM((4, 256, 256), bf16),
            pltpu.VMEM((2, 2, 4, 256, 256), bf16),
            pltpu.VMEM((4, 512, 512), bf16),
            pltpu.VMEM((4, 2, 128, 128), f32),
            pltpu.VMEM((4, 2, 128, 128), f32),
            pltpu.VMEM((32, 64, 128), jnp.int16),
            pltpu.VMEM((32, 64, 128), jnp.int16),
            pltpu.VMEM((32, 1, 128), f32),
            pltpu.VMEM((32, 1, 128), f32),
            pltpu.VMEM((4, 512, 256), bf16),
            pltpu.VMEM((16, 8, 128), f32),
            pltpu.VMEM((16, 32, 3, 8, 128), f32),
            pltpu.VMEM((4, 256, 128), f32),
            pltpu.VMEM((4, 256, 128), f32),
            pltpu.VMEM((2, 256, 128), f32),
            pltpu.VMEM((2, 256, 128), f32),
            pltpu.VMEM((32, 4, 8, 128), f32),
            sem((2,)), sem, sem((2, 32)), sem((2, 32)), sem((2,)), sem((2,)), sem((32,)), sem((32,)),
        ],
        compiler_params=pltpu.CompilerParams(
            collective_id=0, has_side_effects=True, vmem_limit_bytes=60 * 2**20
        ),
    )(transfer_coeffs.transpose(1, 2, 0), transfer_index, spectrum, x_tab, z_tab)
    scalar_field = field.reshape(32, 8, 4, 128).transpose(0, 2, 1, 3).reshape(32, 4, NX)
    rendered = image[:, :32].reshape(8, 4, 4, 32)
    return scalar_field, rendered


def solution(mesh):
    x_tab, z_tab = x_table(), z_table()
    mapped = jax.shard_map(
        body,
        mesh=mesh,
        in_specs=(P(), P(), P(None, "depth", "plane", None), P(), P()),
        out_specs=(P("depth", "plane", None), P(None, None, "plane", "depth")),
        check_vma=False,
    )

    def run(spectrum, transfer_coeffs, transfer_index):
        return mapped(x_tab, z_tab, spectrum, transfer_coeffs, transfer_index)

    return run
```

```python
import math

import jax
import jax.numpy as jnp
import ml_dtypes
import numpy as np
from jax import lax
from jax.experimental import pallas as pl
from jax.experimental.pallas import tpu as pltpu
from jax.sharding import PartitionSpec as P

NX = 1024
NZ = 1024
density = 2.0
shade_gain = 0.4
tau_scale = density / NZ
f32 = jnp.float32
bf16 = jnp.bfloat16
MESH = pl.DeviceIdType.MESH


def split_table(values):
    high = values.astype(ml_dtypes.bfloat16)
    low = (values - high.astype(np.float64)).astype(ml_dtypes.bfloat16)
    return np.stack([high, low])


def x_table():
    k = 4 * np.arange(256)[None, :, None] + np.arange(4)[:, None, None]
    angles = (k * np.arange(256)[None, None, :] % NX) * (2.0 * np.pi / NX)
    tables = [split_table(t / math.sqrt(NX)).reshape(2, 4, 256, 2, 128) for t in (np.cos(angles), np.sin(angles))]
    return np.ascontiguousarray(np.concatenate(tables, axis=4).transpose(3, 0, 1, 2, 4))


def z_table():
    q0 = np.arange(256)
    m = np.arange(256)
    tables = []
    for r in range(4):
        angles = (q0[None, :] * (4 * m[:, None] + r) % NZ) * (2.0 * np.pi / NZ)
        table = np.concatenate([np.cos(angles), -np.sin(angles)], axis=1) / math.sqrt(NZ)
        tables.append(split_table(table).reshape(512, 512))
    return np.stack(tables)


def split(value):
    high = value.astype(bf16)
    return high, (value - high.astype(f32)).astype(bf16)


def dot(a, b):
    return jnp.dot(a, b, preferred_element_type=f32)


def residues(re, im):
    a, b = re[0] + re[2], im[0] + im[2]
    c, d = re[0] - re[2], im[0] - im[2]
    e, f = re[1] + re[3], im[1] + im[3]
    g, h = re[1] - re[3], im[1] - im[3]
    return [(a + e, b + f), (c - h, d + g), (a - e, b - f), (c + h, d - g)]


def lighting(field, before, after, r):
    lane = lax.broadcasted_iota(jnp.int32, field.shape, 1)
    up = pltpu.roll(field, 96, 1)
    down = pltpu.roll(field, 32, 1)
    after = pltpu.roll(after, (96 - 32 * r) % 128, 1) if r != 3 else after
    before = pltpu.roll(before, (-32 * r) % 128, 1) if r else before
    up = jnp.where(lane >= 96, after, up)
    down = jnp.where(lane < 32, before, down)
    return 1.0 + shade_gain * jnp.tanh(0.5 * (up - down))


def coefficients(coeff_ref, index_ref):
    row = lax.broadcasted_iota(jnp.int32, (8, 128), 0)
    result = []
    for channel in range(4):
        for n in range(4):
            value = jnp.zeros((8, 128), f32)
            for image in range(8):
                value = jnp.where(row == image, coeff_ref[channel, n, index_ref[image]], value)
            result.append(value)
    return result


def encode(parts):
    peak = jnp.maximum(jnp.abs(parts[0]), jnp.abs(parts[1]))
    peak = jnp.maximum(jnp.max(peak, axis=0, keepdims=True), 1e-30)
    level = jnp.floor(jnp.log(peak) * (256.0 / math.log(2.0))) + 2.0
    scale = jnp.exp2(level * (-1.0 / 256.0)) * 32766.0
    re, im = (jnp.round(part * scale).astype(jnp.int32) for part in parts)
    return (re << 16) | (im & 0xFFFF), level.astype(jnp.int32)


def decode(codes, level):
    step = jnp.exp2(level.astype(f32) * (1.0 / 256.0)) * (1.0 / 32766.0)
    return (codes >> 16).astype(f32) * step, ((codes << 16) >> 16).astype(f32) * step


def gather_classes(rows_ref, class_ref):
    source = lax.broadcasted_iota(jnp.int32, (256, 256), 0)
    target = lax.broadcasted_iota(jnp.int32, (256, 256), 1)
    move = jnp.where(source == 4 * (target % 64) + target // 64, 1.0, 0.0).astype(bf16)
    low_half = lax.broadcasted_iota(jnp.int32, (256, 128), 1) < 64
    for half in range(2):
        p = [dot(rows_ref[:, 512 * half + 256 * t : 512 * half + 256 * (t + 1)], move) for t in range(2)]
        for j in range(4):
            a, b = (q[:, 128 * (j // 2) : 128 * (j // 2 + 1)] for q in p)
            if j % 2 == 0:
                value = jnp.where(low_half, a, pltpu.roll(b, 64, 1))
            else:
                value = jnp.where(low_half, pltpu.roll(a, 64, 1), b)
            class_ref[j, :, 128 * half : 128 * (half + 1)] = value.astype(bf16)


def softplus(p):
    return jnp.maximum(p, jnp.log(1.0 + jnp.exp(jnp.minimum(p, 80.0))))


def opacity(depth):
    k1, k2, k3 = tau_scale, tau_scale**2 / 2, tau_scale**3 / 6
    small = depth * (k1 - depth * (k2 - depth * k3))
    large = 1.0 - jnp.exp2(depth * (-tau_scale / math.log(2.0)))
    return jnp.where(depth < 16.0, small, large)


def pieces(value, count):
    result = []
    for _ in range(count):
        high = value.astype(bf16)
        result.append(high)
        value = value - high.astype(f32)
    return result


def fill_polynomials(coeffs, poly_ref):
    lane = lax.broadcasted_iota(jnp.int32, (8, 128), 1)
    tables = []
    for channel in range(4):
        terms = []
        for n in (1, 2, 3):
            high, low = (piece.astype(f32) for piece in pieces(coeffs[4 * channel + n], 2))
            terms += [high, high, low, low]
        terms += [piece.astype(f32) for piece in pieces(coeffs[4 * channel], 3)] + [jnp.zeros((8, 128), f32)]
        for tile in range(2):
            value = terms[8 * tile]
            for t in range(1, 8):
                value = jnp.where(lane // 16 == t, terms[8 * tile + t], value)
            tables.append(value)

    @pl.loop(0, 16)
    def _(cell):
        here = lane % 16 == cell
        for pair in range(2):
            rows = pl.ds(pl.multiple_of(cell * 32 + pair * 16, 16), 16)
            for tile in range(2):
                both = [jnp.where(here, tables[2 * (2 * pair + c) + tile], 0.0) for c in range(2)]
                poly_ref[rows, 128 * tile : 128 * (tile + 1)] = jnp.concatenate(both).astype(bf16)


def powers(s):
    result = []
    power = s
    for n in range(3):
        high, low = pieces(power, 2)
        result += [high, low, high, low]
        power = power * s
    return jnp.concatenate(result + [jnp.ones((64, 128), bf16)])


def shuffle(parts, place):
    group = lax.broadcasted_iota(jnp.int32, parts[0].shape, 1) // 32
    result = None
    for g in range(4):
        shift = (32 * (g - place)) % 128
        moved = pltpu.roll(parts[g], shift, 1) if shift else parts[g]
        result = moved if result is None else jnp.where(group == g, moved, result)
    return result


def kernel(
    coeff_ref, index_ref, spectrum_ref, x_hbm, z_hbm,
    field_out, image_out,
    row_ref, class_ref, x_ref, z_ref, wave_ref, mode_ref, send_ref, recv_ref, pair_ref, poly_ref, even_ref, odd_ref, glow_ref, field_ref, light_ref, pack_ref, halo_ref, slab_ref,
    x_sem, z_sem, send_sem, recv_sem, halo_send, halo_recv, slab_send, slab_recv,
):
    me = lax.axis_index("depth")
    plane = lax.axis_index("plane")
    planes = lax.axis_size("plane")
    next_plane = lax.rem(plane + 1, planes)
    last_plane = lax.rem(plane + planes - 1, planes)

    def half_of(step):
        return lax.rem(me // 4 + step, 2)

    def x_copy(step):
        half = half_of(step)
        return pltpu.make_async_copy(x_hbm.at[half], x_ref.at[half], x_sem.at[step])

    z_copy = pltpu.make_async_copy(z_hbm, z_ref, z_sem)

    for step in range(2):
        x_copy(step).start()

    z_copy.start()

    barrier = pltpu.get_barrier_semaphore()

    @pl.loop(1, 32)
    def _(step):
        pl.semaphore_signal(barrier, inc=1, device_id={"depth": lax.rem(me + step, 32)}, device_id_type=MESH)

    pl.semaphore_signal(barrier, inc=1, device_id={"plane": next_plane}, device_id_type=MESH)
    pl.semaphore_signal(barrier, inc=1, device_id={"plane": last_plane}, device_id_type=MESH)

    def mode_send(to):
        return pltpu.make_async_remote_copy(
            src_ref=send_ref.at[to], dst_ref=recv_ref.at[me], send_sem=send_sem.at[to], recv_sem=recv_sem.at[me],
            device_id={"depth": to}, device_id_type=MESH,
        )

    def mode_recv(source):
        return pltpu.make_async_remote_copy(
            src_ref=send_ref.at[source], dst_ref=recv_ref.at[source], send_sem=send_sem.at[source],
            recv_sem=recv_sem.at[source], device_id={"depth": source}, device_id_type=MESH,
        )

    def mode_keep():
        return pltpu.make_async_copy(send_ref.at[me], recv_ref.at[me], recv_sem.at[me])

    row_ref[...] = spectrum_ref[...].reshape(256, NX)
    gather_classes(row_ref, class_ref)

    @pl.loop(0, 2)
    def _(step):
        half = half_of(step)
        x_copy(step).wait()
        for j in range(4):
            waves = dot(class_ref[j], x_ref[half, 0, j]) + dot(class_ref[j], x_ref[half, 1, j])
            wave_ref[j, 0] = waves[:128, :128] - waves[128:, 128:]
            wave_ref[j, 1] = waves[:128, 128:] + waves[128:, :128]
        for k in range(4):
            rows = slice(32 * k, 32 * k + 32)
            re = [wave_ref[j, 0, rows] for j in range(4)]
            im = [wave_ref[j, 1, rows] for j in range(4)]
            for i, pair in enumerate(residues(re, im)):
                mode_ref[i, 0, rows] = pair[0]
                mode_ref[i, 1, rows] = pair[1]

        @pl.when(step == 0)
        def _():
            pl.semaphore_wait(barrier, 33)

        @pl.loop(0, 4)
        def _(turn):
            i = lax.rem(me // 8 + turn + turn // 2 - 2 * (turn // 3), 4)
            first = 8 * i + 4 * half
            parts = [[] for _ in range(4)]
            for part in range(2):
                rows = [mode_ref[i, part, pl.ds(y, 32, stride=4), :] for y in range(4)]
                for d in range(4):
                    parts[d].append(shuffle(rows, d))
            for d in range(4):
                codes, level = encode(parts[d])
                send_ref[first + d, 0:32] = codes
                send_ref[first + d, 32:33] = level

            @pl.loop(0, 4)
            def _(d):
                to = first + d

                @pl.when(to != me)
                def _():
                    mode_send(to).start()

                @pl.when(to == me)
                def _():
                    mode_keep().start()

    fill_polynomials(coefficients(coeff_ref, index_ref), poly_ref)

    @pl.loop(0, 8)
    def _(s):
        @pl.loop(0, 4)
        def _(j):
            source = s + 8 * j

            @pl.when(source != me)
            def _():
                mode_recv(source).wait_recv()

            @pl.when(source == me)
            def _():
                mode_keep().wait()

        re, im = [], []
        for j in range(4):
            real, imag = decode(recv_ref[s + 8 * j, 0:32], recv_ref[s + 8 * j, 32:33])
            re.append(real)
            im.append(imag)
        for r, pair in enumerate(residues(re, im)):
            for part in range(2):
                high, low = split(pair[part])
                rows = pl.ds(pl.multiple_of(part * 256 + s * 32, 32), 32)
                pair_ref[r, rows, 0:128] = high
                pair_ref[r, rows, 128:256] = low

    z_copy.wait()

    @pl.loop(0, 4)
    def _(r):
        p = dot(z_ref[r], pair_ref[r])
        field_ref[r] = (p[:256, :128] + p[:256, 128:]) + (p[256:, :128] + p[256:, 128:])

    @pl.loop(0, 4)
    def _(step):
        rows = pl.ds(pl.multiple_of(step * 64, 64), 64)
        parts = [field_ref[r, rows, :] for r in range(4)]
        pack_ref[0, rows, :] = shuffle(parts, 3)
        pack_ref[1, rows, :] = shuffle(parts, 0)

    halos = [
        pltpu.make_async_remote_copy(
            src_ref=pack_ref.at[side], dst_ref=halo_ref.at[side], send_sem=halo_send.at[side],
            recv_sem=halo_recv.at[side], device_id={"plane": to}, device_id_type=MESH,
        )
        for side, to in ((0, next_plane), (1, last_plane))
    ]
    for halo in halos:
        halo.start()

    def own_rows(slab):
        return field_ref.at[:, pl.ds(pl.multiple_of(slab * 8, 8), 8), :]

    def slab_send_copy(to):
        return pltpu.make_async_remote_copy(
            src_ref=own_rows(to), dst_ref=slab_ref.at[me], send_sem=slab_send.at[to], recv_sem=slab_recv.at[me],
            device_id={"depth": to}, device_id_type=MESH,
        )

    def slab_recv_copy(source):
        return pltpu.make_async_remote_copy(
            src_ref=own_rows(source), dst_ref=slab_ref.at[source], send_sem=slab_send.at[source],
            recv_sem=slab_recv.at[source], device_id={"depth": source}, device_id_type=MESH,
        )

    slab_keep = pltpu.make_async_copy(own_rows(me), slab_ref.at[me], slab_recv.at[me])

    slab_keep.start()

    def evaluate(block, to_ref):
        rows = pl.ds(pl.multiple_of(jnp.minimum(block, 15) * 16, 16), 16)
        for pair in range(2):
            factors = [powers(field_ref[2 * pair + c, rows, :]) for c in range(2)]
            to_ref[pair] = dot(poly_ref[...], jnp.concatenate(factors, axis=1))

    def cell_depths(from_ref, r, k, channel):
        first = 32 * k + 8 * channel
        return softplus(from_ref[r // 2, first : first + 8, 128 * (r % 2) : 128 * (r % 2) + 128])

    def cell_light(block, r, k):
        rows = pl.ds(pl.multiple_of(block * 16, 16), 16)
        return jnp.broadcast_to(light_ref[r, rows, :][k : k + 1, :], (8, 128))

    def absorb(from_ref, r, k, through, depth_sum):
        depth = cell_depths(from_ref, r, k, 3)
        weight = through * opacity(depth)
        return weight, through - weight, depth_sum + depth

    def in_pairs(start, cells, slabs):
        def step(n, state):
            block = start + 2 * n
            if slabs:
                @pl.loop(0, 8)
                def _(k):
                    @pl.when(4 * block + k > 0)
                    def _():
                        slab_send_copy(lax.rem(me + 4 * block + k, 32)).start()

            evaluate(block + 1, odd_ref)
            state = cells(block, even_ref, state)
            evaluate(block + 2, even_ref)
            return cells(block + 1, odd_ref, state)

        return step

    def front(block, from_ref, state):
        through, depth_sum = state
        for k in range(16):
            for r in range(4):
                weight, through, depth_sum = absorb(from_ref, r, k, through, depth_sum)
                for j in range(3):
                    glow_ref[block, 4 * k + r, j] = weight * cell_depths(from_ref, r, k, j)
        return through, depth_sum

    zero = jnp.zeros((8, 128), f32)
    evaluate(0, even_ref)
    through, depth_sum = lax.fori_loop(0, 4, in_pairs(0, front, True), (zero + 1.0, zero))

    for halo in halos:
        halo.wait_recv()

    @pl.loop(0, 8)
    def _(step):
        rows = pl.ds(pl.multiple_of(step * 32, 32), 32)
        for r in range(4):
            light_ref[r, rows, :] = lighting(field_ref[r, rows, :], halo_ref[0, rows, :], halo_ref[1, rows, :], r)

    def lit(block, colors):
        colors = list(colors)
        for k in range(16):
            for r in range(4):
                light = cell_light(block, r, k)
                for j in range(3):
                    colors[j] = colors[j] + light * glow_ref[block, 4 * k + r, j]
        return tuple(colors)

    colors = lax.fori_loop(0, 8, lit, (zero, zero, zero))

    def back(block, from_ref, state):
        *colors, through, depth_sum = state
        for k in range(16):
            for r in range(4):
                weight, through, depth_sum = absorb(from_ref, r, k, through, depth_sum)
                weight = weight * cell_light(block, r, k)
                for j in range(3):
                    colors[j] = colors[j] + weight * cell_depths(from_ref, r, k, j)
        return (*colors, through, depth_sum)

    c0, c1, c2, _, depth_sum = lax.fori_loop(0, 4, in_pairs(8, back, False), (*colors, through, depth_sum))
    for channel, image in enumerate((c0, c1, c2, jnp.exp(depth_sum * -tau_scale))):
        for y in range(4):
            moved = pltpu.roll(image, 128 - 32 * y, 1) if y else image
            image_out[pl.ds(channel * 4 + y, 8, stride=16), :] = moved

    slab_keep.wait()

    @pl.loop(1, 32)
    def _(step):
        slab_recv_copy(lax.rem(me + step, 32)).wait_recv()

    @pl.loop(0, 8)
    def _(g):
        for r in range(4):
            parts = [slab_ref[g * 4 + d, r] for d in range(4)]
            for y in range(4):
                field_out[pl.ds(r * 32 + g * 4 + y, 8, stride=128), :] = shuffle(parts, y)

    @pl.loop(1, 32)
    def _(step):
        to = lax.rem(me + step, 32)
        mode_send(to).wait_send()
        slab_send_copy(to).wait_send()

    for halo in halos:
        halo.wait_send()


def body(x_tab, z_tab, spectrum, transfer_coeffs, transfer_index):
    smem = pl.BlockSpec(memory_space=pltpu.SMEM)
    vmem = pl.BlockSpec(memory_space=pltpu.VMEM)
    hbm = pl.BlockSpec(memory_space=pl.ANY)
    sem = pltpu.SemaphoreType.DMA
    field, image = pl.pallas_call(
        kernel,
        out_shape=[jax.ShapeDtypeStruct((1024, 128), f32), jax.ShapeDtypeStruct((128, 128), f32)],
        in_specs=[smem, smem, vmem, hbm, hbm],
        out_specs=[vmem, vmem],
        scratch_shapes=[
            pltpu.VMEM((256, NX), bf16),
            pltpu.VMEM((4, 256, 256), bf16),
            pltpu.VMEM((2, 2, 4, 256, 256), bf16),
            pltpu.VMEM((4, 512, 512), bf16),
            pltpu.VMEM((4, 2, 128, 128), f32),
            pltpu.VMEM((4, 2, 128, 128), f32),
            pltpu.VMEM((32, 33, 128), jnp.int32),
            pltpu.VMEM((32, 33, 128), jnp.int32),
            pltpu.VMEM((4, 512, 256), bf16),
            pltpu.VMEM((512, 256), bf16),
            pltpu.VMEM((2, 512, 256), f32),
            pltpu.VMEM((2, 512, 256), f32),
            pltpu.VMEM((8, 64, 3, 8, 128), f32),
            pltpu.VMEM((4, 256, 128), f32),
            pltpu.VMEM((4, 256, 128), f32),
            pltpu.VMEM((2, 256, 128), f32),
            pltpu.VMEM((2, 256, 128), f32),
            pltpu.VMEM((32, 4, 8, 128), f32),
            sem((2,)), sem, sem((32,)), sem((32,)), sem((2,)), sem((2,)), sem((32,)), sem((32,)),
        ],
        compiler_params=pltpu.CompilerParams(
            collective_id=0, has_side_effects=True, vmem_limit_bytes=60 * 2**20
        ),
    )(transfer_coeffs.transpose(1, 2, 0), transfer_index, spectrum, x_tab, z_tab)
    scalar_field = field.reshape(32, 8, 4, 128).transpose(0, 2, 1, 3).reshape(32, 4, NX)
    rendered = image[:, :32].reshape(8, 4, 4, 32)
    return scalar_field, rendered


def solution(mesh):
    x_tab, z_tab = x_table(), z_table()
    mapped = jax.shard_map(
        body,
        mesh=mesh,
        in_specs=(P(), P(), P(None, "depth", "plane", None), P(), P()),
        out_specs=(P("depth", "plane", None), P(None, None, "plane", "depth")),
        check_vma=False,
    )

    def run(spectrum, transfer_coeffs, transfer_index):
        return mapped(x_tab, z_tab, spectrum, transfer_coeffs, transfer_index)

    return run
```

```python
import math

import jax
import jax.numpy as jnp
import ml_dtypes
import numpy as np
from jax import lax
from jax.experimental import pallas as pl
from jax.experimental.pallas import tpu as pltpu
from jax.sharding import PartitionSpec as P

NX = 1024
NZ = 1024
density = 2.0
shade_gain = 0.4
tau_scale = density / NZ
f32 = jnp.float32
bf16 = jnp.bfloat16
MESH = pl.DeviceIdType.MESH


def split_table(values):
    high = values.astype(ml_dtypes.bfloat16)
    low = (values - high.astype(np.float64)).astype(ml_dtypes.bfloat16)
    return np.stack([high, low])


def x_table():
    k = 4 * np.arange(256)[None, :, None] + np.arange(4)[:, None, None]
    angles = (k * np.arange(256)[None, None, :] % NX) * (2.0 * np.pi / NX)
    tables = [split_table(t / math.sqrt(NX)).reshape(2, 4, 256, 2, 128) for t in (np.cos(angles), np.sin(angles))]
    return np.ascontiguousarray(np.concatenate(tables, axis=4).transpose(3, 0, 1, 2, 4))


def z_table():
    q0 = np.arange(256)
    m = np.arange(256)
    tables = []
    for r in range(4):
        angles = (q0[None, :] * (4 * m[:, None] + r) % NZ) * (2.0 * np.pi / NZ)
        table = np.concatenate([np.cos(angles), -np.sin(angles)], axis=1) / math.sqrt(NZ)
        tables.append(split_table(table).reshape(512, 512))
    return np.stack(tables)


def split(value):
    high = value.astype(bf16)
    return high, (value - high.astype(f32)).astype(bf16)


def dot(a, b):
    return jnp.dot(a, b, preferred_element_type=f32)


def residues(re, im):
    a, b = re[0] + re[2], im[0] + im[2]
    c, d = re[0] - re[2], im[0] - im[2]
    e, f = re[1] + re[3], im[1] + im[3]
    g, h = re[1] - re[3], im[1] - im[3]
    return [(a + e, b + f), (c - h, d + g), (a - e, b - f), (c + h, d - g)]


def lighting(field, before, after, r):
    lane = lax.broadcasted_iota(jnp.int32, field.shape, 1)
    up = pltpu.roll(field, 96, 1)
    down = pltpu.roll(field, 32, 1)
    after = pltpu.roll(after, (96 - 32 * r) % 128, 1) if r != 3 else after
    before = pltpu.roll(before, (-32 * r) % 128, 1) if r else before
    up = jnp.where(lane >= 96, after, up)
    down = jnp.where(lane < 32, before, down)
    return 1.0 + shade_gain * jnp.tanh(0.5 * (up - down))


def coefficients(coeff_ref, index_ref):
    row = lax.broadcasted_iota(jnp.int32, (8, 128), 0)
    result = []
    for channel in range(4):
        for n in range(4):
            value = jnp.zeros((8, 128), f32)
            for image in range(8):
                value = jnp.where(row == image, coeff_ref[channel, n, index_ref[image]], value)
            result.append(value)
    return result


def encode(parts):
    peak = jnp.maximum(jnp.abs(parts[0]), jnp.abs(parts[1]))
    peak = jnp.maximum(jnp.max(peak, axis=0, keepdims=True), 1e-30)
    level = jnp.floor(jnp.log(peak) * (256.0 / math.log(2.0))) + 2.0
    scale = jnp.exp2(level * (-1.0 / 256.0)) * 32766.0
    re, im = (jnp.round(part * scale).astype(jnp.int32) for part in parts)
    return (re << 16) | (im & 0xFFFF), level.astype(jnp.int32)


def decode(codes, level):
    step = jnp.exp2(level.astype(f32) * (1.0 / 256.0)) * (1.0 / 32766.0)
    return (codes >> 16).astype(f32) * step, ((codes << 16) >> 16).astype(f32) * step


def gather_classes(rows_ref, class_ref):
    source = lax.broadcasted_iota(jnp.int32, (256, 256), 0)
    target = lax.broadcasted_iota(jnp.int32, (256, 256), 1)
    move = jnp.where(source == 4 * (target % 64) + target // 64, 1.0, 0.0).astype(bf16)
    low_half = lax.broadcasted_iota(jnp.int32, (256, 128), 1) < 64
    for half in range(2):
        p = [dot(rows_ref[:, 512 * half + 256 * t : 512 * half + 256 * (t + 1)], move) for t in range(2)]
        for j in range(4):
            a, b = (q[:, 128 * (j // 2) : 128 * (j // 2 + 1)] for q in p)
            if j % 2 == 0:
                value = jnp.where(low_half, a, pltpu.roll(b, 64, 1))
            else:
                value = jnp.where(low_half, pltpu.roll(a, 64, 1), b)
            class_ref[j, :, 128 * half : 128 * (half + 1)] = value.astype(bf16)


def softplus(p):
    return jnp.maximum(p, jnp.log(1.0 + jnp.exp(jnp.minimum(p, 80.0))))


def opacity(depth):
    k1, k2, k3 = tau_scale, tau_scale**2 / 2, tau_scale**3 / 6
    small = depth * (k1 - depth * (k2 - depth * k3))
    large = 1.0 - jnp.exp2(depth * (-tau_scale / math.log(2.0)))
    return jnp.where(depth < 16.0, small, large)


def pieces(value, count):
    result = []
    for _ in range(count):
        high = value.astype(bf16)
        result.append(high)
        value = value - high.astype(f32)
    return result


def fill_polynomials(coeffs, poly_ref):
    lane = lax.broadcasted_iota(jnp.int32, (8, 128), 1)
    tables = []
    for channel in range(4):
        terms = []
        for n in (1, 2, 3):
            high, low = (piece.astype(f32) for piece in pieces(coeffs[4 * channel + n], 2))
            terms += [high, high, low, low]
        terms += [piece.astype(f32) for piece in pieces(coeffs[4 * channel], 3)] + [jnp.zeros((8, 128), f32)]
        for tile in range(2):
            value = terms[8 * tile]
            for t in range(1, 8):
                value = jnp.where(lane // 16 == t, terms[8 * tile + t], value)
            tables.append(value)

    @pl.loop(0, 16)
    def _(cell):
        here = lane % 16 == cell
        for pair in range(2):
            rows = pl.ds(pl.multiple_of(cell * 32 + pair * 16, 16), 16)
            for tile in range(2):
                both = [jnp.where(here, tables[2 * (2 * pair + c) + tile], 0.0) for c in range(2)]
                poly_ref[rows, 128 * tile : 128 * (tile + 1)] = jnp.concatenate(both).astype(bf16)


def powers(s):
    result = []
    power = s
    for n in range(3):
        high, low = pieces(power, 2)
        result += [high, low, high, low]
        power = power * s
    return jnp.concatenate(result + [jnp.ones((64, 128), bf16)])


def shuffle(parts, place):
    group = lax.broadcasted_iota(jnp.int32, parts[0].shape, 1) // 32
    result = None
    for g in range(4):
        shift = (32 * (g - place)) % 128
        moved = pltpu.roll(parts[g], shift, 1) if shift else parts[g]
        result = moved if result is None else jnp.where(group == g, moved, result)
    return result


def kernel(
    coeff_hbm, index_hbm, spectrum_hbm, x_hbm, z_hbm,
    field_out, image_out,
    coeff_ref, index_ref, spectrum_ref, row_ref, class_ref, x_ref, z_ref, wave_ref, mode_ref, send_ref, recv_ref, pair_ref, poly_ref, even_ref, odd_ref, glow_ref, field_ref, light_ref, pack_ref, halo_ref, slab_ref,
    in_sem, x_sem, z_sem, send_sem, recv_sem, halo_send, halo_recv, slab_send, slab_recv,
):
    me = lax.axis_index("depth")
    plane = lax.axis_index("plane")
    planes = lax.axis_size("plane")
    next_plane = lax.rem(plane + 1, planes)
    last_plane = lax.rem(plane + planes - 1, planes)

    def half_of(step):
        return lax.rem(me // 4 + step, 2)

    def x_copy(step):
        half = half_of(step)
        return pltpu.make_async_copy(x_hbm.at[half], x_ref.at[half], x_sem.at[step])

    z_copy = pltpu.make_async_copy(z_hbm, z_ref, z_sem)
    spectrum_copy = pltpu.make_async_copy(spectrum_hbm, spectrum_ref, in_sem.at[0])
    small_copies = [
        pltpu.make_async_copy(coeff_hbm, coeff_ref, in_sem.at[1]),
        pltpu.make_async_copy(index_hbm, index_ref, in_sem.at[2]),
    ]
    spectrum_copy.start()

    for step in range(2):
        x_copy(step).start()

    z_copy.start()
    for copy in small_copies:
        copy.start()

    barrier = pltpu.get_barrier_semaphore()

    @pl.loop(1, 32)
    def _(step):
        pl.semaphore_signal(barrier, inc=1, device_id={"depth": lax.rem(me + step, 32)}, device_id_type=MESH)

    pl.semaphore_signal(barrier, inc=1, device_id={"plane": next_plane}, device_id_type=MESH)
    pl.semaphore_signal(barrier, inc=1, device_id={"plane": last_plane}, device_id_type=MESH)

    def mode_send(to):
        return pltpu.make_async_remote_copy(
            src_ref=send_ref.at[to], dst_ref=recv_ref.at[me], send_sem=send_sem.at[to], recv_sem=recv_sem.at[me],
            device_id={"depth": to}, device_id_type=MESH,
        )

    def mode_recv(source):
        return pltpu.make_async_remote_copy(
            src_ref=send_ref.at[source], dst_ref=recv_ref.at[source], send_sem=send_sem.at[source],
            recv_sem=recv_sem.at[source], device_id={"depth": source}, device_id_type=MESH,
        )

    def mode_keep():
        return pltpu.make_async_copy(send_ref.at[me], recv_ref.at[me], recv_sem.at[me])

    spectrum_copy.wait()
    row_ref[...] = spectrum_ref[...].reshape(256, NX)
    gather_classes(row_ref, class_ref)

    @pl.loop(0, 2)
    def _(step):
        half = half_of(step)
        x_copy(step).wait()
        for j in range(4):
            waves = dot(class_ref[j], x_ref[half, 0, j]) + dot(class_ref[j], x_ref[half, 1, j])
            wave_ref[j, 0] = waves[:128, :128] - waves[128:, 128:]
            wave_ref[j, 1] = waves[:128, 128:] + waves[128:, :128]
        for k in range(4):
            rows = slice(32 * k, 32 * k + 32)
            re = [wave_ref[j, 0, rows] for j in range(4)]
            im = [wave_ref[j, 1, rows] for j in range(4)]
            for i, pair in enumerate(residues(re, im)):
                mode_ref[i, 0, rows] = pair[0]
                mode_ref[i, 1, rows] = pair[1]

        @pl.when(step == 0)
        def _():
            pl.semaphore_wait(barrier, 33)

        @pl.loop(0, 4)
        def _(turn):
            i = lax.rem(me // 8 + turn + turn // 2 - 2 * (turn // 3), 4)
            first = 8 * i + 4 * half
            parts = [[] for _ in range(4)]
            for part in range(2):
                rows = [mode_ref[i, part, pl.ds(y, 32, stride=4), :] for y in range(4)]
                for d in range(4):
                    parts[d].append(shuffle(rows, d))
            for d in range(4):
                codes, level = encode(parts[d])
                send_ref[first + d, 0:32] = codes
                send_ref[first + d, 32:33] = level

            @pl.loop(0, 4)
            def _(d):
                to = first + d

                @pl.when(to != me)
                def _():
                    mode_send(to).start()

                @pl.when(to == me)
                def _():
                    mode_keep().start()

    for copy in small_copies:
        copy.wait()
    fill_polynomials(coefficients(coeff_ref, index_ref), poly_ref)

    @pl.loop(0, 8)
    def _(s):
        @pl.loop(0, 4)
        def _(j):
            source = s + 8 * j

            @pl.when(source != me)
            def _():
                mode_recv(source).wait_recv()

            @pl.when(source == me)
            def _():
                mode_keep().wait()

        re, im = [], []
        for j in range(4):
            real, imag = decode(recv_ref[s + 8 * j, 0:32], recv_ref[s + 8 * j, 32:33])
            re.append(real)
            im.append(imag)
        for r, pair in enumerate(residues(re, im)):
            for part in range(2):
                high, low = split(pair[part])
                rows = pl.ds(pl.multiple_of(part * 256 + s * 32, 32), 32)
                pair_ref[r, rows, 0:128] = high
                pair_ref[r, rows, 128:256] = low

    z_copy.wait()

    @pl.loop(0, 4)
    def _(r):
        p = dot(z_ref[r], pair_ref[r])
        field_ref[r] = (p[:256, :128] + p[:256, 128:]) + (p[256:, :128] + p[256:, 128:])

    @pl.loop(0, 4)
    def _(step):
        rows = pl.ds(pl.multiple_of(step * 64, 64), 64)
        parts = [field_ref[r, rows, :] for r in range(4)]
        pack_ref[0, rows, :] = shuffle(parts, 3)
        pack_ref[1, rows, :] = shuffle(parts, 0)

    halos = [
        pltpu.make_async_remote_copy(
            src_ref=pack_ref.at[side], dst_ref=halo_ref.at[side], send_sem=halo_send.at[side],
            recv_sem=halo_recv.at[side], device_id={"plane": to}, device_id_type=MESH,
        )
        for side, to in ((0, next_plane), (1, last_plane))
    ]
    for halo in halos:
        halo.start()

    def own_rows(slab):
        return field_ref.at[:, pl.ds(pl.multiple_of(slab * 8, 8), 8), :]

    def slab_send_copy(to):
        return pltpu.make_async_remote_copy(
            src_ref=own_rows(to), dst_ref=slab_ref.at[me], send_sem=slab_send.at[to], recv_sem=slab_recv.at[me],
            device_id={"depth": to}, device_id_type=MESH,
        )

    def slab_recv_copy(source):
        return pltpu.make_async_remote_copy(
            src_ref=own_rows(source), dst_ref=slab_ref.at[source], send_sem=slab_send.at[source],
            recv_sem=slab_recv.at[source], device_id={"depth": source}, device_id_type=MESH,
        )

    slab_keep = pltpu.make_async_copy(own_rows(me), slab_ref.at[me], slab_recv.at[me])

    slab_keep.start()

    @pl.loop(1, 32)
    def _(step):
        slab_send_copy(lax.rem(me + step, 32)).start()

    def evaluate(block, to_ref):
        rows = pl.ds(pl.multiple_of(jnp.minimum(block, 15) * 16, 16), 16)
        for pair in range(2):
            factors = [powers(field_ref[2 * pair + c, rows, :]) for c in range(2)]
            to_ref[pair] = dot(poly_ref[...], jnp.concatenate(factors, axis=1))

    def cell_depths(from_ref, r, k, channel):
        first = 32 * k + 8 * channel
        return softplus(from_ref[r // 2, first : first + 8, 128 * (r % 2) : 128 * (r % 2) + 128])

    def cell_light(block, r, k):
        rows = pl.ds(pl.multiple_of(block * 16, 16), 16)
        return jnp.broadcast_to(light_ref[r, rows, :][k : k + 1, :], (8, 128))

    def absorb(from_ref, r, k, through, depth_sum):
        depth = cell_depths(from_ref, r, k, 3)
        weight = through * opacity(depth)
        return weight, through - weight, depth_sum + depth

    def join_slabs(g):
        for r in range(4):
            parts = [slab_ref[g * 4 + d, r] for d in range(4)]
            for y in range(4):
                field_out[pl.ds(r * 32 + g * 4 + y, 8, stride=128), :] = shuffle(parts, y)

    def in_pairs(start, cells, join):
        def step(n, state):
            block = start + 2 * n
            groups = [lax.rem(me // 4 + 15 - 2 * n - k, 8) for k in range(2)] if join else []
            for g in groups:

                @pl.loop(0, 4)
                def _(d):
                    source = 4 * g + d

                    @pl.when(source != me)
                    def _():
                        slab_recv_copy(source).wait_recv()

                    @pl.when(source == me)
                    def _():
                        slab_keep.wait()

            evaluate(block + 1, odd_ref)
            state = cells(block, even_ref, state)
            for g in groups:
                join_slabs(g)
            evaluate(block + 2, even_ref)
            return cells(block + 1, odd_ref, state)

        return step

    def front(block, from_ref, state):
        through, depth_sum = state
        for k in range(16):
            for r in range(4):
                weight, through, depth_sum = absorb(from_ref, r, k, through, depth_sum)
                for j in range(3):
                    glow_ref[block, 4 * k + r, j] = weight * cell_depths(from_ref, r, k, j)
        return through, depth_sum

    zero = jnp.zeros((8, 128), f32)
    evaluate(0, even_ref)
    through, depth_sum = lax.fori_loop(0, 4, in_pairs(0, front, False), (zero + 1.0, zero))

    for halo in halos:
        halo.wait_recv()

    @pl.loop(0, 8)
    def _(step):
        rows = pl.ds(pl.multiple_of(step * 32, 32), 32)
        for r in range(4):
            light_ref[r, rows, :] = lighting(field_ref[r, rows, :], halo_ref[0, rows, :], halo_ref[1, rows, :], r)

    def lit(block, colors):
        colors = list(colors)
        for k in range(16):
            for r in range(4):
                light = cell_light(block, r, k)
                for j in range(3):
                    colors[j] = colors[j] + light * glow_ref[block, 4 * k + r, j]
        return tuple(colors)

    colors = lax.fori_loop(0, 8, lit, (zero, zero, zero))

    def back(block, from_ref, state):
        *colors, through, depth_sum = state
        for k in range(16):
            for r in range(4):
                weight, through, depth_sum = absorb(from_ref, r, k, through, depth_sum)
                weight = weight * cell_light(block, r, k)
                for j in range(3):
                    colors[j] = colors[j] + weight * cell_depths(from_ref, r, k, j)
        return (*colors, through, depth_sum)

    c0, c1, c2, _, depth_sum = lax.fori_loop(0, 4, in_pairs(8, back, True), (*colors, through, depth_sum))
    for channel, image in enumerate((c0, c1, c2, jnp.exp(depth_sum * -tau_scale))):
        for y in range(4):
            moved = pltpu.roll(image, 128 - 32 * y, 1) if y else image
            image_out[pl.ds(channel * 4 + y, 8, stride=16), :] = moved

    @pl.loop(1, 32)
    def _(step):
        to = lax.rem(me + step, 32)
        mode_send(to).wait_send()
        slab_send_copy(to).wait_send()

    for halo in halos:
        halo.wait_send()


def body(x_tab, z_tab, spectrum, transfer_coeffs, transfer_index):
    vmem = pl.BlockSpec(memory_space=pltpu.VMEM)
    hbm = pl.BlockSpec(memory_space=pl.ANY)
    sem = pltpu.SemaphoreType.DMA
    field, image = pl.pallas_call(
        kernel,
        out_shape=[jax.ShapeDtypeStruct((1024, 128), f32), jax.ShapeDtypeStruct((128, 128), f32)],
        in_specs=[hbm] * 5,
        out_specs=[vmem, vmem],
        scratch_shapes=[
            pltpu.SMEM((4, 4, 8), f32),
            pltpu.SMEM((8,), jnp.int32),
            pltpu.VMEM((2, 32, 4, NX), bf16),
            pltpu.VMEM((256, NX), bf16),
            pltpu.VMEM((4, 256, 256), bf16),
            pltpu.VMEM((2, 2, 4, 256, 256), bf16),
            pltpu.VMEM((4, 512, 512), bf16),
            pltpu.VMEM((4, 2, 128, 128), f32),
            pltpu.VMEM((4, 2, 128, 128), f32),
            pltpu.VMEM((32, 33, 128), jnp.int32),
            pltpu.VMEM((32, 33, 128), jnp.int32),
            pltpu.VMEM((4, 512, 256), bf16),
            pltpu.VMEM((512, 256), bf16),
            pltpu.VMEM((2, 512, 256), f32),
            pltpu.VMEM((2, 512, 256), f32),
            pltpu.VMEM((8, 64, 3, 8, 128), f32),
            pltpu.VMEM((4, 256, 128), f32),
            pltpu.VMEM((4, 256, 128), f32),
            pltpu.VMEM((2, 256, 128), f32),
            pltpu.VMEM((2, 256, 128), f32),
            pltpu.VMEM((32, 4, 8, 128), f32),
            sem((3,)), sem((2,)), sem, sem((32,)), sem((32,)), sem((2,)), sem((2,)), sem((32,)), sem((32,)),
        ],
        compiler_params=pltpu.CompilerParams(
            collective_id=0, has_side_effects=True, vmem_limit_bytes=60 * 2**20
        ),
    )(transfer_coeffs.transpose(1, 2, 0), transfer_index, spectrum, x_tab, z_tab)
    scalar_field = field.reshape(32, 8, 4, 128).transpose(0, 2, 1, 3).reshape(32, 4, NX)
    rendered = image[:, :32].reshape(8, 4, 4, 32)
    return scalar_field, rendered


def solution(mesh):
    x_tab, z_tab = x_table(), z_table()
    mapped = jax.shard_map(
        body,
        mesh=mesh,
        in_specs=(P(), P(), P(None, "depth", "plane", None), P(), P()),
        out_specs=(P("depth", "plane", None), P(None, None, "plane", "depth")),
        check_vma=False,
    )

    def run(spectrum, transfer_coeffs, transfer_index):
        return mapped(x_tab, z_tab, spectrum, transfer_coeffs, transfer_index)

    return run
```

```python
import math

import jax
import jax.numpy as jnp
import ml_dtypes
import numpy as np
from jax import lax
from jax.experimental import pallas as pl
from jax.experimental.pallas import tpu as pltpu
from jax.sharding import PartitionSpec as P

NX = 1024
NZ = 1024
density = 2.0
shade_gain = 0.4
tau_scale = density / NZ
LN2 = math.log(2.0)
f32 = jnp.float32
bf16 = jnp.bfloat16
MESH = pl.DeviceIdType.MESH


def split_table(values):
    high = values.astype(ml_dtypes.bfloat16)
    low = (values - high.astype(np.float64)).astype(ml_dtypes.bfloat16)
    return np.stack([high, low])


def x_table():
    k = 4 * np.arange(256)[None, :, None] + np.arange(4)[:, None, None]
    angles = (k * np.arange(256)[None, None, :] % NX) * (2.0 * np.pi / NX)
    tables = [split_table(t / math.sqrt(NX)).reshape(2, 4, 256, 2, 128) for t in (np.cos(angles), np.sin(angles))]
    return np.ascontiguousarray(np.concatenate(tables, axis=4).transpose(3, 0, 1, 2, 4))


def z_table():
    q0 = np.arange(256)
    m = np.arange(256)
    tables = []
    for r in range(4):
        angles = (q0[None, :] * (4 * m[:, None] + r) % NZ) * (2.0 * np.pi / NZ)
        table = np.concatenate([np.cos(angles), -np.sin(angles)], axis=1) / math.sqrt(NZ)
        tables.append(split_table(table).reshape(512, 512))
    return np.stack(tables)


def split(value):
    high = value.astype(bf16)
    return high, (value - high.astype(f32)).astype(bf16)


def dot(a, b):
    return jnp.dot(a, b, preferred_element_type=f32)


def residues(re, im):
    a, b = re[0] + re[2], im[0] + im[2]
    c, d = re[0] - re[2], im[0] - im[2]
    e, f = re[1] + re[3], im[1] + im[3]
    g, h = re[1] - re[3], im[1] - im[3]
    return [(a + e, b + f), (c - h, d + g), (a - e, b - f), (c + h, d - g)]


def lighting(field, before, after, r):
    lane = lax.broadcasted_iota(jnp.int32, field.shape, 1)
    up = pltpu.roll(field, 96, 1)
    down = pltpu.roll(field, 32, 1)
    after = pltpu.roll(after, (96 - 32 * r) % 128, 1) if r != 3 else after
    before = pltpu.roll(before, (-32 * r) % 128, 1) if r else before
    up = jnp.where(lane >= 96, after, up)
    down = jnp.where(lane < 32, before, down)
    return 1.0 + shade_gain * jnp.tanh(0.5 * (up - down))


def coefficients(coeff_ref, index_ref):
    row = lax.broadcasted_iota(jnp.int32, (8, 128), 0)
    result = []
    for channel in range(4):
        for n in range(4):
            value = jnp.zeros((8, 128), f32)
            for image in range(8):
                value = jnp.where(row == image, coeff_ref[channel, n, index_ref[image]], value)
            result.append(value)
    return result


def encode(parts):
    peak = jnp.maximum(jnp.abs(parts[0]), jnp.abs(parts[1]))
    peak = jnp.maximum(jnp.max(peak, axis=0, keepdims=True), 1e-30)
    level = jnp.floor(jnp.log(peak) * (256.0 / math.log(2.0))) + 2.0
    scale = jnp.exp2(level * (-1.0 / 256.0)) * 32766.0
    re, im = (jnp.round(part * scale).astype(jnp.int32) for part in parts)
    return (re << 16) | (im & 0xFFFF), level.astype(jnp.int32)


def decode(codes, level):
    step = jnp.exp2(level.astype(f32) * (1.0 / 256.0)) * (1.0 / 32766.0)
    return (codes >> 16).astype(f32) * step, ((codes << 16) >> 16).astype(f32) * step


def gather_classes(rows_ref, class_ref):
    source = lax.broadcasted_iota(jnp.int32, (256, 256), 0)
    target = lax.broadcasted_iota(jnp.int32, (256, 256), 1)
    move = jnp.where(source == 4 * (target % 64) + target // 64, 1.0, 0.0).astype(bf16)
    low_half = lax.broadcasted_iota(jnp.int32, (256, 128), 1) < 64
    for half in range(2):
        p = [dot(rows_ref[:, 512 * half + 256 * t : 512 * half + 256 * (t + 1)], move) for t in range(2)]
        for j in range(4):
            a, b = (q[:, 128 * (j // 2) : 128 * (j // 2 + 1)] for q in p)
            if j % 2 == 0:
                value = jnp.where(low_half, a, pltpu.roll(b, 64, 1))
            else:
                value = jnp.where(low_half, pltpu.roll(a, 64, 1), b)
            class_ref[j, :, 128 * half : 128 * (half + 1)] = value.astype(bf16)


def softplus(p):
    return jnp.maximum(p, jnp.log2(1.0 + jnp.exp2(jnp.minimum(p, 120.0))))


def opacity(depth):
    k = LN2 * tau_scale
    small = depth * (k - depth * (k * k / 2))
    large = 1.0 - jnp.exp2(depth * -tau_scale)
    return jnp.where(depth < 2.5, small, large)


def pieces(value, count):
    result = []
    for _ in range(count):
        high = value.astype(bf16)
        result.append(high)
        value = value - high.astype(f32)
    return result


def fill_polynomials(coeffs, poly_ref):
    lane = lax.broadcasted_iota(jnp.int32, (8, 128), 1)
    tables = []
    for channel in range(4):
        terms = []
        for n in (1, 2, 3):
            high, low = (piece.astype(f32) for piece in pieces(coeffs[4 * channel + n] * (1.0 / LN2), 2))
            terms += [high, high, low, low]
        terms += [piece.astype(f32) for piece in pieces(coeffs[4 * channel] * (1.0 / LN2), 3)] + [jnp.zeros((8, 128), f32)]
        for tile in range(2):
            value = terms[8 * tile]
            for t in range(1, 8):
                value = jnp.where(lane // 16 == t, terms[8 * tile + t], value)
            tables.append(value)

    @pl.loop(0, 16)
    def _(cell):
        here = lane % 16 == cell
        for pair in range(2):
            rows = pl.ds(pl.multiple_of(cell * 32 + pair * 16, 16), 16)
            for tile in range(2):
                both = [jnp.where(here, tables[2 * (2 * pair + c) + tile], 0.0) for c in range(2)]
                poly_ref[rows, 128 * tile : 128 * (tile + 1)] = jnp.concatenate(both).astype(bf16)


def powers(s):
    result = []
    power = s
    for n in range(3):
        high, low = pieces(power, 2)
        result += [high, low, high, low]
        power = power * s
    return jnp.concatenate(result + [jnp.ones((64, 128), bf16)])


def shuffle(parts, place):
    group = lax.broadcasted_iota(jnp.int32, parts[0].shape, 1) // 32
    result = None
    for g in range(4):
        shift = (32 * (g - place)) % 128
        moved = pltpu.roll(parts[g], shift, 1) if shift else parts[g]
        result = moved if result is None else jnp.where(group == g, moved, result)
    return result


def kernel(
    coeff_hbm, index_hbm, spectrum_hbm, x_hbm, z_hbm,
    field_out, image_out,
    coeff_ref, index_ref, spectrum_ref, row_ref, class_ref, x_ref, z_ref, wave_ref, mode_ref, send_ref, recv_ref, pair_ref, poly_ref, even_ref, odd_ref, glow_ref, field_ref, light_ref, pack_ref, halo_ref, slab_ref,
    in_sem, x_sem, z_sem, send_sem, recv_sem, halo_send, halo_recv, slab_send, slab_recv,
):
    me = lax.axis_index("depth")
    plane = lax.axis_index("plane")
    planes = lax.axis_size("plane")
    next_plane = lax.rem(plane + 1, planes)
    last_plane = lax.rem(plane + planes - 1, planes)

    def half_of(step):
        return lax.rem(me // 4 + step, 2)

    def x_copy(step):
        half = half_of(step)
        return pltpu.make_async_copy(x_hbm.at[half], x_ref.at[half], x_sem.at[step])

    z_copy = pltpu.make_async_copy(z_hbm, z_ref, z_sem)
    spectrum_copy = pltpu.make_async_copy(spectrum_hbm, spectrum_ref, in_sem.at[0])
    small_copies = [
        pltpu.make_async_copy(coeff_hbm, coeff_ref, in_sem.at[1]),
        pltpu.make_async_copy(index_hbm, index_ref, in_sem.at[2]),
    ]
    spectrum_copy.start()

    for step in range(2):
        x_copy(step).start()

    z_copy.start()
    for copy in small_copies:
        copy.start()

    barrier = pltpu.get_barrier_semaphore()

    @pl.loop(1, 32)
    def _(step):
        pl.semaphore_signal(barrier, inc=1, device_id={"depth": lax.rem(me + step, 32)}, device_id_type=MESH)

    pl.semaphore_signal(barrier, inc=1, device_id={"plane": next_plane}, device_id_type=MESH)
    pl.semaphore_signal(barrier, inc=1, device_id={"plane": last_plane}, device_id_type=MESH)

    def mode_send(to):
        return pltpu.make_async_remote_copy(
            src_ref=send_ref.at[to], dst_ref=recv_ref.at[me], send_sem=send_sem.at[to], recv_sem=recv_sem.at[me],
            device_id={"depth": to}, device_id_type=MESH,
        )

    def mode_recv(source):
        return pltpu.make_async_remote_copy(
            src_ref=send_ref.at[source], dst_ref=recv_ref.at[source], send_sem=send_sem.at[source],
            recv_sem=recv_sem.at[source], device_id={"depth": source}, device_id_type=MESH,
        )

    def mode_keep():
        return pltpu.make_async_copy(send_ref.at[me], recv_ref.at[me], recv_sem.at[me])

    spectrum_copy.wait()
    row_ref[...] = spectrum_ref[...].reshape(256, NX)
    gather_classes(row_ref, class_ref)

    @pl.loop(0, 2)
    def _(step):
        half = half_of(step)
        x_copy(step).wait()
        for j in range(4):
            waves = dot(class_ref[j], x_ref[half, 0, j]) + dot(class_ref[j], x_ref[half, 1, j])
            wave_ref[j, 0] = waves[:128, :128] - waves[128:, 128:]
            wave_ref[j, 1] = waves[:128, 128:] + waves[128:, :128]
        for k in range(4):
            rows = slice(32 * k, 32 * k + 32)
            re = [wave_ref[j, 0, rows] for j in range(4)]
            im = [wave_ref[j, 1, rows] for j in range(4)]
            for i, pair in enumerate(residues(re, im)):
                mode_ref[i, 0, rows] = pair[0]
                mode_ref[i, 1, rows] = pair[1]

        @pl.when(step == 0)
        def _():
            pl.semaphore_wait(barrier, 33)

        @pl.loop(0, 4)
        def _(turn):
            i = lax.rem(me // 8 + turn + turn // 2 - 2 * (turn // 3), 4)
            first = 8 * i + 4 * half
            parts = [[] for _ in range(4)]
            for part in range(2):
                rows = [mode_ref[i, part, pl.ds(y, 32, stride=4), :] for y in range(4)]
                for d in range(4):
                    parts[d].append(shuffle(rows, d))
            for d in range(4):
                codes, level = encode(parts[d])
                send_ref[first + d, 0:32] = codes
                send_ref[first + d, 32:33] = level

            @pl.loop(0, 4)
            def _(d):
                to = first + d

                @pl.when(to != me)
                def _():
                    mode_send(to).start()

                @pl.when(to == me)
                def _():
                    mode_keep().start()

    for copy in small_copies:
        copy.wait()
    fill_polynomials(coefficients(coeff_ref, index_ref), poly_ref)

    @pl.loop(0, 8)
    def _(s):
        @pl.loop(0, 4)
        def _(j):
            source = s + 8 * j

            @pl.when(source != me)
            def _():
                mode_recv(source).wait_recv()

            @pl.when(source == me)
            def _():
                mode_keep().wait()

        re, im = [], []
        for j in range(4):
            real, imag = decode(recv_ref[s + 8 * j, 0:32], recv_ref[s + 8 * j, 32:33])
            re.append(real)
            im.append(imag)
        for r, pair in enumerate(residues(re, im)):
            for part in range(2):
                high, low = split(pair[part])
                rows = pl.ds(pl.multiple_of(part * 256 + s * 32, 32), 32)
                pair_ref[r, rows, 0:128] = high
                pair_ref[r, rows, 128:256] = low

    z_copy.wait()

    @pl.loop(0, 4)
    def _(r):
        p = dot(z_ref[r], pair_ref[r])
        field_ref[r] = (p[:256, :128] + p[:256, 128:]) + (p[256:, :128] + p[256:, 128:])

    @pl.loop(0, 4)
    def _(step):
        rows = pl.ds(pl.multiple_of(step * 64, 64), 64)
        parts = [field_ref[r, rows, :] for r in range(4)]
        pack_ref[0, rows, :] = shuffle(parts, 3)
        pack_ref[1, rows, :] = shuffle(parts, 0)

    halos = [
        pltpu.make_async_remote_copy(
            src_ref=pack_ref.at[side], dst_ref=halo_ref.at[side], send_sem=halo_send.at[side],
            recv_sem=halo_recv.at[side], device_id={"plane": to}, device_id_type=MESH,
        )
        for side, to in ((0, next_plane), (1, last_plane))
    ]
    for halo in halos:
        halo.start()

    def own_rows(slab):
        return field_ref.at[:, pl.ds(pl.multiple_of(slab * 8, 8), 8), :]

    def slab_send_copy(to):
        return pltpu.make_async_remote_copy(
            src_ref=own_rows(to), dst_ref=slab_ref.at[me], send_sem=slab_send.at[to], recv_sem=slab_recv.at[me],
            device_id={"depth": to}, device_id_type=MESH,
        )

    def slab_recv_copy(source):
        return pltpu.make_async_remote_copy(
            src_ref=own_rows(source), dst_ref=slab_ref.at[source], send_sem=slab_send.at[source],
            recv_sem=slab_recv.at[source], device_id={"depth": source}, device_id_type=MESH,
        )

    slab_keep = pltpu.make_async_copy(own_rows(me), slab_ref.at[me], slab_recv.at[me])

    slab_keep.start()

    @pl.loop(1, 32)
    def _(step):
        slab_send_copy(lax.rem(me + step, 32)).start()

    def evaluate(block, to_ref):
        rows = pl.ds(pl.multiple_of(jnp.minimum(block, 15) * 16, 16), 16)
        for pair in range(2):
            factors = [powers(field_ref[2 * pair + c, rows, :]) for c in range(2)]
            to_ref[pair] = dot(poly_ref[...], jnp.concatenate(factors, axis=1))

    def cell_depths(from_ref, r, k, channel):
        first = 32 * k + 8 * channel
        return softplus(from_ref[r // 2, first : first + 8, 128 * (r % 2) : 128 * (r % 2) + 128])

    def cell_light(block, r, k):
        rows = pl.ds(pl.multiple_of(block * 16, 16), 16)
        return jnp.broadcast_to(light_ref[r, rows, :][k : k + 1, :], (8, 128))

    def absorb(from_ref, r, k, through):
        weight = through * opacity(cell_depths(from_ref, r, k, 3))
        return weight, through - weight

    def join_slabs(g):
        for r in range(4):
            parts = [slab_ref[g * 4 + d, r] for d in range(4)]
            for y in range(4):
                field_out[pl.ds(r * 32 + g * 4 + y, 8, stride=128), :] = shuffle(parts, y)

    def in_fours(start, cells, join):
        def step(n, state):
            block = start + 4 * n
            groups = [lax.rem(me // 4 + 15 - 4 * n - k, 8) for k in range(4)] if join else []
            for g in groups:

                @pl.loop(0, 4)
                def _(d):
                    source = 4 * g + d

                    @pl.when(source != me)
                    def _():
                        slab_recv_copy(source).wait_recv()

                    @pl.when(source == me)
                    def _():
                        slab_keep.wait()

            for k in range(4):
                here, ahead = (even_ref, odd_ref) if k % 2 == 0 else (odd_ref, even_ref)
                evaluate(block + k + 1, ahead)
                state = cells(block + k, here, state)
                for g in groups[k : k + 1]:
                    join_slabs(g)
            return state

        return step

    def front(block, from_ref, state):
        through = state
        for k in range(16):
            for r in range(4):
                weight, through = absorb(from_ref, r, k, through)
                for j in range(3):
                    glow_ref[block, 4 * k + r, j] = weight * cell_depths(from_ref, r, k, j)
        return through

    zero = jnp.zeros((8, 128), f32)
    evaluate(0, even_ref)
    through = lax.fori_loop(0, 2, in_fours(0, front, False), zero + 1.0)

    for halo in halos:
        halo.wait_recv()

    @pl.loop(0, 8)
    def _(step):
        rows = pl.ds(pl.multiple_of(step * 32, 32), 32)
        for r in range(4):
            light_ref[r, rows, :] = lighting(field_ref[r, rows, :], halo_ref[0, rows, :], halo_ref[1, rows, :], r)

    def lit(block, colors):
        colors = list(colors)
        for k in range(16):
            for r in range(4):
                light = cell_light(block, r, k)
                for j in range(3):
                    colors[j] = colors[j] + light * glow_ref[block, 4 * k + r, j]
        return tuple(colors)

    colors = lax.fori_loop(0, 8, lit, (zero, zero, zero))

    def back(block, from_ref, state):
        *colors, through = state
        for k in range(16):
            for r in range(4):
                weight, through = absorb(from_ref, r, k, through)
                weight = weight * cell_light(block, r, k)
                for j in range(3):
                    colors[j] = colors[j] + weight * cell_depths(from_ref, r, k, j)
        return (*colors, through)

    *colors, through = lax.fori_loop(0, 2, in_fours(8, back, True), (*colors, through))
    for channel, image in enumerate([color * LN2 for color in colors] + [through]):
        for y in range(4):
            moved = pltpu.roll(image, 128 - 32 * y, 1) if y else image
            image_out[pl.ds(channel * 4 + y, 8, stride=16), :] = moved

    @pl.loop(1, 32)
    def _(step):
        to = lax.rem(me + step, 32)
        mode_send(to).wait_send()
        slab_send_copy(to).wait_send()

    for halo in halos:
        halo.wait_send()


def body(x_tab, z_tab, spectrum, transfer_coeffs, transfer_index):
    vmem = pl.BlockSpec(memory_space=pltpu.VMEM)
    hbm = pl.BlockSpec(memory_space=pl.ANY)
    sem = pltpu.SemaphoreType.DMA
    field, image = pl.pallas_call(
        kernel,
        out_shape=[jax.ShapeDtypeStruct((1024, 128), f32), jax.ShapeDtypeStruct((128, 128), f32)],
        in_specs=[hbm] * 5,
        out_specs=[vmem, vmem],
        scratch_shapes=[
            pltpu.SMEM((4, 4, 8), f32),
            pltpu.SMEM((8,), jnp.int32),
            pltpu.VMEM((2, 32, 4, NX), bf16),
            pltpu.VMEM((256, NX), bf16),
            pltpu.VMEM((4, 256, 256), bf16),
            pltpu.VMEM((2, 2, 4, 256, 256), bf16),
            pltpu.VMEM((4, 512, 512), bf16),
            pltpu.VMEM((4, 2, 128, 128), f32),
            pltpu.VMEM((4, 2, 128, 128), f32),
            pltpu.VMEM((32, 33, 128), jnp.int32),
            pltpu.VMEM((32, 33, 128), jnp.int32),
            pltpu.VMEM((4, 512, 256), bf16),
            pltpu.VMEM((512, 256), bf16),
            pltpu.VMEM((2, 512, 256), f32),
            pltpu.VMEM((2, 512, 256), f32),
            pltpu.VMEM((8, 64, 3, 8, 128), f32),
            pltpu.VMEM((4, 256, 128), f32),
            pltpu.VMEM((4, 256, 128), f32),
            pltpu.VMEM((2, 256, 128), f32),
            pltpu.VMEM((2, 256, 128), f32),
            pltpu.VMEM((32, 4, 8, 128), f32),
            sem((3,)), sem((2,)), sem, sem((32,)), sem((32,)), sem((2,)), sem((2,)), sem((32,)), sem((32,)),
        ],
        compiler_params=pltpu.CompilerParams(
            collective_id=0, has_side_effects=True, vmem_limit_bytes=53 * 2**20
        ),
    )(transfer_coeffs.transpose(1, 2, 0), transfer_index, spectrum, x_tab, z_tab)
    scalar_field = field.reshape(32, 8, 4, 128).transpose(0, 2, 1, 3).reshape(32, 4, NX)
    rendered = image[:, :32].reshape(8, 4, 4, 32)
    return scalar_field, rendered


def solution(mesh):
    x_tab, z_tab = x_table(), z_table()
    mapped = jax.shard_map(
        body,
        mesh=mesh,
        in_specs=(P(), P(), P(None, "depth", "plane", None), P(), P()),
        out_specs=(P("depth", "plane", None), P(None, None, "plane", "depth")),
        check_vma=False,
    )

    def run(spectrum, transfer_coeffs, transfer_index):
        return mapped(x_tab, z_tab, spectrum, transfer_coeffs, transfer_index)

    return run
```

```python
import math

import jax
import jax.numpy as jnp
import ml_dtypes
import numpy as np
from jax import lax
from jax.experimental import pallas as pl
from jax.experimental.pallas import tpu as pltpu
from jax.sharding import PartitionSpec as P

NX = 1024
NZ = 1024
density = 2.0
shade_gain = 0.4
tau_scale = density / NZ
LN2 = math.log(2.0)
f32 = jnp.float32
bf16 = jnp.bfloat16
MESH = pl.DeviceIdType.MESH


def split_table(values):
    high = values.astype(ml_dtypes.bfloat16)
    low = (values - high.astype(np.float64)).astype(ml_dtypes.bfloat16)
    return np.stack([high, low])


def x_table():
    k = 4 * np.arange(256)[None, :, None] + np.arange(4)[:, None, None]
    angles = (k * np.arange(256)[None, None, :] % NX) * (2.0 * np.pi / NX)
    tables = [split_table(t / math.sqrt(NX)).reshape(2, 4, 256, 2, 128) for t in (np.cos(angles), np.sin(angles))]
    return np.ascontiguousarray(np.concatenate(tables, axis=4).transpose(3, 0, 1, 2, 4))


def z_table():
    q0 = np.arange(256)
    m = np.arange(256)
    tables = []
    for r in range(4):
        angles = (q0[None, :] * (4 * m[:, None] + r) % NZ) * (2.0 * np.pi / NZ)
        table = np.concatenate([np.cos(angles), -np.sin(angles)], axis=1) / math.sqrt(NZ)
        tables.append(split_table(table).reshape(512, 512))
    return np.stack(tables)


def split(value):
    high = value.astype(bf16)
    return high, (value - high.astype(f32)).astype(bf16)


def dot(a, b):
    return jnp.dot(a, b, preferred_element_type=f32)


def residues(re, im):
    a, b = re[0] + re[2], im[0] + im[2]
    c, d = re[0] - re[2], im[0] - im[2]
    e, f = re[1] + re[3], im[1] + im[3]
    g, h = re[1] - re[3], im[1] - im[3]
    return [(a + e, b + f), (c - h, d + g), (a - e, b - f), (c + h, d - g)]


def lighting(field, before, after, r):
    lane = lax.broadcasted_iota(jnp.int32, field.shape, 1)
    up = pltpu.roll(field, 96, 1)
    down = pltpu.roll(field, 32, 1)
    after = pltpu.roll(after, (96 - 32 * r) % 128, 1) if r != 3 else after
    before = pltpu.roll(before, (-32 * r) % 128, 1) if r else before
    up = jnp.where(lane >= 96, after, up)
    down = jnp.where(lane < 32, before, down)
    return 1.0 + shade_gain * jnp.tanh(0.5 * (up - down))


def coefficients(coeff_ref, index_ref):
    row = lax.broadcasted_iota(jnp.int32, (8, 128), 0)
    result = []
    for channel in range(4):
        for n in range(4):
            value = jnp.zeros((8, 128), f32)
            for image in range(8):
                value = jnp.where(row == image, coeff_ref[channel, n, index_ref[image]], value)
            result.append(value)
    return result


def encode(parts):
    peak = jnp.maximum(jnp.abs(parts[0]), jnp.abs(parts[1]))
    peak = jnp.maximum(jnp.max(peak, axis=0, keepdims=True), 1e-30)
    level = jnp.floor(jnp.log(peak) * (256.0 / math.log(2.0))) + 2.0
    scale = jnp.exp2(level * (-1.0 / 256.0)) * 32766.0
    re, im = (jnp.round(part * scale).astype(jnp.int32) for part in parts)
    return (re << 16) | (im & 0xFFFF), level.astype(jnp.int32)


def decode(codes, level):
    step = jnp.exp2(level.astype(f32) * (1.0 / 256.0)) * (1.0 / 32766.0)
    return (codes >> 16).astype(f32) * step, ((codes << 16) >> 16).astype(f32) * step


def gather_classes(rows_ref, class_ref):
    source = lax.broadcasted_iota(jnp.int32, (256, 256), 0)
    target = lax.broadcasted_iota(jnp.int32, (256, 256), 1)
    move = jnp.where(source == 4 * (target % 64) + target // 64, 1.0, 0.0).astype(bf16)
    low_half = lax.broadcasted_iota(jnp.int32, (256, 128), 1) < 64
    for half in range(2):
        p = [dot(rows_ref[:, 512 * half + 256 * t : 512 * half + 256 * (t + 1)], move) for t in range(2)]
        for j in range(4):
            a, b = (q[:, 128 * (j // 2) : 128 * (j // 2 + 1)] for q in p)
            if j % 2 == 0:
                value = jnp.where(low_half, a, pltpu.roll(b, 64, 1))
            else:
                value = jnp.where(low_half, pltpu.roll(a, 64, 1), b)
            class_ref[j, :, 128 * half : 128 * (half + 1)] = value.astype(bf16)


def softplus(p):
    return jnp.maximum(p, jnp.log2(1.0 + jnp.exp2(jnp.minimum(p, 120.0))))


def opacity(depth):
    k = LN2 * tau_scale
    small = depth * (k - depth * (k * k / 2))
    large = 1.0 - jnp.exp2(depth * -tau_scale)
    return jnp.where(depth < 2.5, small, large)


def pieces(value, count):
    result = []
    for _ in range(count):
        high = value.astype(bf16)
        result.append(high)
        value = value - high.astype(f32)
    return result


def fill_polynomials(coeffs, poly_ref):
    lane = lax.broadcasted_iota(jnp.int32, (8, 128), 1)
    tables = []
    for channel in range(4):
        terms = []
        for n in (1, 2, 3):
            high, low = (piece.astype(f32) for piece in pieces(coeffs[4 * channel + n] * (1.0 / LN2), 2))
            terms += [high, high, low, low]
        terms += [piece.astype(f32) for piece in pieces(coeffs[4 * channel] * (1.0 / LN2), 3)] + [jnp.zeros((8, 128), f32)]
        for tile in range(2):
            value = terms[8 * tile]
            for t in range(1, 8):
                value = jnp.where(lane // 16 == t, terms[8 * tile + t], value)
            tables.append(value)

    @pl.loop(0, 16)
    def _(cell):
        here = lane % 16 == cell
        for pair in range(2):
            rows = pl.ds(pl.multiple_of(cell * 32 + pair * 16, 16), 16)
            for tile in range(2):
                both = [jnp.where(here, tables[2 * (2 * pair + c) + tile], 0.0) for c in range(2)]
                poly_ref[rows, 128 * tile : 128 * (tile + 1)] = jnp.concatenate(both).astype(bf16)


def powers(s):
    result = []
    power = s
    for n in range(3):
        high, low = pieces(power, 2)
        result += [high, low, high, low]
        power = power * s
    return jnp.concatenate(result + [jnp.ones((64, 128), bf16)])


def shuffle(parts, place):
    group = lax.broadcasted_iota(jnp.int32, parts[0].shape, 1) // 32
    result = None
    for g in range(4):
        shift = (32 * (g - place)) % 128
        moved = pltpu.roll(parts[g], shift, 1) if shift else parts[g]
        result = moved if result is None else jnp.where(group == g, moved, result)
    return result


def kernel(
    coeff_hbm, index_hbm, spectrum_hbm, x_hbm, z_hbm,
    field_out, image_out,
    coeff_ref, index_ref, spectrum_ref, row_ref, class_ref, x_ref, z_ref, wave_ref, mode_ref, send_ref, recv_ref, pair_ref, poly_ref, even_ref, odd_ref, glow_ref, field_ref, light_ref, pack_ref, halo_ref, slab_ref,
    in_sem, x_sem, z_sem, send_sem, recv_sem, halo_send, halo_recv, slab_send, slab_recv,
):
    me = lax.axis_index("depth")
    plane = lax.axis_index("plane")
    planes = lax.axis_size("plane")
    next_plane = lax.rem(plane + 1, planes)
    last_plane = lax.rem(plane + planes - 1, planes)

    def half_of(step):
        return lax.rem(me // 4 + step, 2)

    def x_copy(step):
        half = half_of(step)
        return pltpu.make_async_copy(x_hbm.at[half], x_ref.at[half], x_sem.at[step])

    z_copy = pltpu.make_async_copy(z_hbm, z_ref, z_sem)
    spectrum_copy = pltpu.make_async_copy(spectrum_hbm, spectrum_ref, in_sem.at[0])
    small_copies = [
        pltpu.make_async_copy(coeff_hbm, coeff_ref, in_sem.at[1]),
        pltpu.make_async_copy(index_hbm, index_ref, in_sem.at[2]),
    ]
    spectrum_copy.start()

    for step in range(2):
        x_copy(step).start()

    z_copy.start()
    for copy in small_copies:
        copy.start()

    barrier = pltpu.get_barrier_semaphore()

    @pl.loop(1, 32)
    def _(step):
        pl.semaphore_signal(barrier, inc=1, device_id={"depth": lax.rem(me + step, 32)}, device_id_type=MESH)

    pl.semaphore_signal(barrier, inc=1, device_id={"plane": next_plane}, device_id_type=MESH)
    pl.semaphore_signal(barrier, inc=1, device_id={"plane": last_plane}, device_id_type=MESH)

    def mode_send(to):
        return pltpu.make_async_remote_copy(
            src_ref=send_ref.at[to], dst_ref=recv_ref.at[me], send_sem=send_sem.at[to], recv_sem=recv_sem.at[me],
            device_id={"depth": to}, device_id_type=MESH,
        )

    def mode_recv(source):
        return pltpu.make_async_remote_copy(
            src_ref=send_ref.at[source], dst_ref=recv_ref.at[source], send_sem=send_sem.at[source],
            recv_sem=recv_sem.at[source], device_id={"depth": source}, device_id_type=MESH,
        )

    def mode_keep():
        return pltpu.make_async_copy(send_ref.at[me], recv_ref.at[me], recv_sem.at[me])

    spectrum_copy.wait()
    row_ref[...] = spectrum_ref[...].reshape(256, NX)
    gather_classes(row_ref, class_ref)

    @pl.loop(0, 2)
    def _(step):
        half = half_of(step)
        x_copy(step).wait()
        for j in range(4):
            waves = dot(class_ref[j], x_ref[half, 0, j]) + dot(class_ref[j], x_ref[half, 1, j])
            wave_ref[j, 0] = waves[:128, :128] - waves[128:, 128:]
            wave_ref[j, 1] = waves[:128, 128:] + waves[128:, :128]
        for k in range(4):
            rows = slice(32 * k, 32 * k + 32)
            re = [wave_ref[j, 0, rows] for j in range(4)]
            im = [wave_ref[j, 1, rows] for j in range(4)]
            for i, pair in enumerate(residues(re, im)):
                mode_ref[i, 0, rows] = pair[0]
                mode_ref[i, 1, rows] = pair[1]

        @pl.when(step == 0)
        def _():
            pl.semaphore_wait(barrier, 33)

        @pl.loop(0, 4)
        def _(turn):
            i = lax.rem(me // 8 + turn + turn // 2 - 2 * (turn // 3), 4)
            first = 8 * i + 4 * half
            parts = [[] for _ in range(4)]
            for part in range(2):
                rows = [mode_ref[i, part, pl.ds(y, 32, stride=4), :] for y in range(4)]
                for d in range(4):
                    parts[d].append(shuffle(rows, d))
            for d in range(4):
                codes, level = encode(parts[d])
                send_ref[first + d, 0:32] = codes
                send_ref[first + d, 32:33] = level

            @pl.loop(0, 4)
            def _(d):
                to = first + d

                @pl.when(to != me)
                def _():
                    mode_send(to).start()

                @pl.when(to == me)
                def _():
                    mode_keep().start()

    for copy in small_copies:
        copy.wait()
    fill_polynomials(coefficients(coeff_ref, index_ref), poly_ref)

    @pl.loop(0, 8)
    def _(s):
        @pl.loop(0, 4)
        def _(j):
            source = s + 8 * j

            @pl.when(source != me)
            def _():
                mode_recv(source).wait_recv()

            @pl.when(source == me)
            def _():
                mode_keep().wait()

        re, im = [], []
        for j in range(4):
            real, imag = decode(recv_ref[s + 8 * j, 0:32], recv_ref[s + 8 * j, 32:33])
            re.append(real)
            im.append(imag)
        for r, pair in enumerate(residues(re, im)):
            for part in range(2):
                high, low = split(pair[part])
                rows = pl.ds(pl.multiple_of(part * 256 + s * 32, 32), 32)
                pair_ref[r, rows, 0:128] = high
                pair_ref[r, rows, 128:256] = low

    z_copy.wait()

    @pl.loop(0, 4)
    def _(r):
        p = dot(z_ref[r], pair_ref[r])
        field_ref[r] = (p[:256, :128] + p[:256, 128:]) + (p[256:, :128] + p[256:, 128:])

    @pl.loop(0, 4)
    def _(step):
        rows = pl.ds(pl.multiple_of(step * 64, 64), 64)
        parts = [field_ref[r, rows, :] for r in range(4)]
        pack_ref[0, rows, :] = shuffle(parts, 3)
        pack_ref[1, rows, :] = shuffle(parts, 0)

    halos = [
        pltpu.make_async_remote_copy(
            src_ref=pack_ref.at[side], dst_ref=halo_ref.at[side], send_sem=halo_send.at[side],
            recv_sem=halo_recv.at[side], device_id={"plane": to}, device_id_type=MESH,
        )
        for side, to in ((0, next_plane), (1, last_plane))
    ]
    for halo in halos:
        halo.start()

    def own_rows(slab):
        return field_ref.at[:, pl.ds(pl.multiple_of(slab * 8, 8), 8), :]

    def slab_send_copy(to):
        return pltpu.make_async_remote_copy(
            src_ref=own_rows(to), dst_ref=slab_ref.at[me], send_sem=slab_send.at[to], recv_sem=slab_recv.at[me],
            device_id={"depth": to}, device_id_type=MESH,
        )

    def slab_recv_copy(source):
        return pltpu.make_async_remote_copy(
            src_ref=own_rows(source), dst_ref=slab_ref.at[source], send_sem=slab_send.at[source],
            recv_sem=slab_recv.at[source], device_id={"depth": source}, device_id_type=MESH,
        )

    slab_keep = pltpu.make_async_copy(own_rows(me), slab_ref.at[me], slab_recv.at[me])

    slab_keep.start()

    @pl.loop(1, 32)
    def _(step):
        slab_send_copy(lax.rem(me + step, 32)).start()

    def evaluate(block, to_ref):
        rows = pl.ds(pl.multiple_of(jnp.minimum(block, 15) * 16, 16), 16)
        for pair in range(2):
            factors = [powers(field_ref[2 * pair + c, rows, :]) for c in range(2)]
            to_ref[pair] = dot(poly_ref[...], jnp.concatenate(factors, axis=1))

    def cell_depths(from_ref, r, k, channel):
        first = 32 * k + 8 * channel
        return softplus(from_ref[r // 2, first : first + 8, 128 * (r % 2) : 128 * (r % 2) + 128])

    def cell_light(block, r, k):
        rows = pl.ds(pl.multiple_of(block * 16, 16), 16)
        return jnp.broadcast_to(light_ref[r, rows, :][k : k + 1, :], (8, 128))

    def absorb(from_ref, r, k, through):
        weight = through * opacity(cell_depths(from_ref, r, k, 3))
        return weight, through - weight

    def join_slabs(g):
        for r in range(4):
            parts = [slab_ref[g * 4 + d, r] for d in range(4)]
            for y in range(4):
                field_out[pl.ds(r * 32 + g * 4 + y, 8, stride=128), :] = shuffle(parts, y)

    def in_fours(start, cells, join):
        def step(n, state):
            block = start + 4 * n
            groups = [lax.rem(me // 4 + 15 - k, 8) for k in range(8)] if join else []
            for g in groups:

                @pl.loop(0, 4)
                def _(d):
                    source = 4 * g + d

                    @pl.when(source != me)
                    def _():
                        slab_recv_copy(source).wait_recv()

                    @pl.when(source == me)
                    def _():
                        slab_keep.wait()

            for k in range(4):
                here, ahead = (even_ref, odd_ref) if k % 2 == 0 else (odd_ref, even_ref)
                evaluate(block + k + 1, ahead)
                state = cells(block + k, here, state)
                for g in groups[2 * k : 2 * k + 2]:
                    join_slabs(g)
            return state

        return step

    def front(block, from_ref, state):
        through = state
        for k in range(16):
            for r in range(4):
                weight, through = absorb(from_ref, r, k, through)
                for j in range(3):
                    glow_ref[block, 4 * k + r, j] = weight * cell_depths(from_ref, r, k, j)
        return through

    zero = jnp.zeros((8, 128), f32)
    evaluate(0, even_ref)
    through = lax.fori_loop(0, 3, in_fours(0, front, False), zero + 1.0)

    for halo in halos:
        halo.wait_recv()

    @pl.loop(0, 4)
    def _(step):
        rows = pl.ds(pl.multiple_of(step * 64, 64), 64)
        for r in range(4):
            light_ref[r, rows, :] = lighting(field_ref[r, rows, :], halo_ref[0, rows, :], halo_ref[1, rows, :], r)

    def lit(block, colors):
        colors = list(colors)
        for k in range(16):
            for r in range(4):
                light = cell_light(block, r, k)
                for j in range(3):
                    colors[j] = colors[j] + light * glow_ref[block, 4 * k + r, j]
        return tuple(colors)

    colors = lax.fori_loop(0, 12, lit, (zero, zero, zero))

    def back(block, from_ref, state):
        *colors, through = state
        for k in range(16):
            for r in range(4):
                weight, through = absorb(from_ref, r, k, through)
                weight = weight * cell_light(block, r, k)
                for j in range(3):
                    colors[j] = colors[j] + weight * cell_depths(from_ref, r, k, j)
        return (*colors, through)

    *colors, through = in_fours(12, back, True)(0, (*colors, through))
    for channel, image in enumerate([color * LN2 for color in colors] + [through]):
        for y in range(4):
            moved = pltpu.roll(image, 128 - 32 * y, 1) if y else image
            image_out[pl.ds(channel * 4 + y, 8, stride=16), :] = moved

    @pl.loop(1, 32)
    def _(step):
        to = lax.rem(me + step, 32)
        mode_send(to).wait_send()
        slab_send_copy(to).wait_send()

    for halo in halos:
        halo.wait_send()


def body(x_tab, z_tab, spectrum, transfer_coeffs, transfer_index):
    vmem = pl.BlockSpec(memory_space=pltpu.VMEM)
    hbm = pl.BlockSpec(memory_space=pl.ANY)
    sem = pltpu.SemaphoreType.DMA
    field, image = pl.pallas_call(
        kernel,
        out_shape=[jax.ShapeDtypeStruct((1024, 128), f32), jax.ShapeDtypeStruct((128, 128), f32)],
        in_specs=[hbm] * 5,
        out_specs=[vmem, vmem],
        scratch_shapes=[
            pltpu.SMEM((4, 4, 8), f32),
            pltpu.SMEM((8,), jnp.int32),
            pltpu.VMEM((2, 32, 4, NX), bf16),
            pltpu.VMEM((256, NX), bf16),
            pltpu.VMEM((4, 256, 256), bf16),
            pltpu.VMEM((2, 2, 4, 256, 256), bf16),
            pltpu.VMEM((4, 512, 512), bf16),
            pltpu.VMEM((4, 2, 128, 128), f32),
            pltpu.VMEM((4, 2, 128, 128), f32),
            pltpu.VMEM((32, 33, 128), jnp.int32),
            pltpu.VMEM((32, 33, 128), jnp.int32),
            pltpu.VMEM((4, 512, 256), bf16),
            pltpu.VMEM((512, 256), bf16),
            pltpu.VMEM((2, 512, 256), f32),
            pltpu.VMEM((2, 512, 256), f32),
            pltpu.VMEM((12, 64, 3, 8, 128), f32),
            pltpu.VMEM((4, 256, 128), f32),
            pltpu.VMEM((4, 256, 128), f32),
            pltpu.VMEM((2, 256, 128), f32),
            pltpu.VMEM((2, 256, 128), f32),
            pltpu.VMEM((32, 4, 8, 128), f32),
            sem((3,)), sem((2,)), sem, sem((32,)), sem((32,)), sem((2,)), sem((2,)), sem((32,)), sem((32,)),
        ],
        compiler_params=pltpu.CompilerParams(
            collective_id=0, has_side_effects=True, vmem_limit_bytes=53 * 2**20
        ),
    )(transfer_coeffs.transpose(1, 2, 0), transfer_index, spectrum, x_tab, z_tab)
    scalar_field = field.reshape(32, 8, 4, 128).transpose(0, 2, 1, 3).reshape(32, 4, NX)
    rendered = image[:, :32].reshape(8, 4, 4, 32)
    return scalar_field, rendered


def solution(mesh):
    x_tab, z_tab = x_table(), z_table()
    mapped = jax.shard_map(
        body,
        mesh=mesh,
        in_specs=(P(), P(), P(None, "depth", "plane", None), P(), P()),
        out_specs=(P("depth", "plane", None), P(None, None, "plane", "depth")),
        check_vma=False,
    )

    def run(spectrum, transfer_coeffs, transfer_index):
        return mapped(x_tab, z_tab, spectrum, transfer_coeffs, transfer_index)

    return run
```

```python
import math

import jax
import jax.numpy as jnp
import ml_dtypes
import numpy as np
from jax import lax
from jax.experimental import pallas as pl
from jax.experimental.pallas import tpu as pltpu
from jax.sharding import PartitionSpec as P

NX = 1024
NZ = 1024
density = 2.0
shade_gain = 0.4
tau_scale = density / NZ
LN2 = math.log(2.0)
f32 = jnp.float32
bf16 = jnp.bfloat16
MESH = pl.DeviceIdType.MESH


def split_table(values):
    high = values.astype(ml_dtypes.bfloat16)
    low = (values - high.astype(np.float64)).astype(ml_dtypes.bfloat16)
    return np.stack([high, low])


def x_table():
    k = 4 * np.arange(256)[None, :, None] + np.arange(4)[:, None, None]
    angles = (k * np.arange(256)[None, None, :] % NX) * (2.0 * np.pi / NX)
    tables = [split_table(t / math.sqrt(NX)).reshape(2, 4, 256, 2, 128) for t in (np.cos(angles), np.sin(angles))]
    return np.ascontiguousarray(np.concatenate(tables, axis=4).transpose(3, 0, 1, 2, 4))


def z_table():
    q0 = np.arange(256)
    m = np.arange(256)
    tables = []
    for r in range(4):
        angles = (q0[None, :] * (4 * m[:, None] + r) % NZ) * (2.0 * np.pi / NZ)
        table = np.concatenate([np.cos(angles), -np.sin(angles)], axis=1) / math.sqrt(NZ)
        tables.append(split_table(table).reshape(512, 512))
    return np.stack(tables)


def split(value):
    high = value.astype(bf16)
    return high, (value - high.astype(f32)).astype(bf16)


def dot(a, b):
    return jnp.dot(a, b, preferred_element_type=f32)


def residues(re, im):
    a, b = re[0] + re[2], im[0] + im[2]
    c, d = re[0] - re[2], im[0] - im[2]
    e, f = re[1] + re[3], im[1] + im[3]
    g, h = re[1] - re[3], im[1] - im[3]
    return [(a + e, b + f), (c - h, d + g), (a - e, b - f), (c + h, d - g)]


def lighting(field, before, after, r):
    lane = lax.broadcasted_iota(jnp.int32, field.shape, 1)
    up = pltpu.roll(field, 96, 1)
    down = pltpu.roll(field, 32, 1)
    after = pltpu.roll(after, (96 - 32 * r) % 128, 1) if r != 3 else after
    before = pltpu.roll(before, (-32 * r) % 128, 1) if r else before
    up = jnp.where(lane >= 96, after, up)
    down = jnp.where(lane < 32, before, down)
    return 1.0 + shade_gain * jnp.tanh(0.5 * (up - down))


def coefficients(coeff_ref, index_ref):
    row = lax.broadcasted_iota(jnp.int32, (8, 128), 0)
    result = []
    for channel in range(4):
        for n in range(4):
            value = jnp.zeros((8, 128), f32)
            for image in range(8):
                value = jnp.where(row == image, coeff_ref[channel, n, index_ref[image]], value)
            result.append(value)
    return result


def encode(parts):
    peak = jnp.maximum(jnp.abs(parts[0]), jnp.abs(parts[1]))
    peak = jnp.maximum(jnp.max(peak, axis=0, keepdims=True), 1e-30)
    level = jnp.floor(jnp.log(peak) * (256.0 / math.log(2.0))) + 2.0
    scale = jnp.exp2(level * (-1.0 / 256.0)) * 32766.0
    re, im = (jnp.round(part * scale).astype(jnp.int32) for part in parts)
    return (re << 16) | (im & 0xFFFF), level.astype(jnp.int32)


def decode(codes, level):
    step = jnp.exp2(level.astype(f32) * (1.0 / 256.0)) * (1.0 / 32766.0)
    return (codes >> 16).astype(f32) * step, ((codes << 16) >> 16).astype(f32) * step


def gather_classes(rows_ref, class_ref):
    source = lax.broadcasted_iota(jnp.int32, (256, 256), 0)
    target = lax.broadcasted_iota(jnp.int32, (256, 256), 1)
    move = jnp.where(source == 4 * (target % 64) + target // 64, 1.0, 0.0).astype(bf16)
    low_half = lax.broadcasted_iota(jnp.int32, (256, 128), 1) < 64
    for half in range(2):
        p = [dot(rows_ref[:, 512 * half + 256 * t : 512 * half + 256 * (t + 1)], move) for t in range(2)]
        for j in range(4):
            a, b = (q[:, 128 * (j // 2) : 128 * (j // 2 + 1)] for q in p)
            if j % 2 == 0:
                value = jnp.where(low_half, a, pltpu.roll(b, 64, 1))
            else:
                value = jnp.where(low_half, pltpu.roll(a, 64, 1), b)
            class_ref[j, :, 128 * half : 128 * (half + 1)] = value.astype(bf16)


def softplus(p):
    return jnp.maximum(p, jnp.log2(1.0 + jnp.exp2(jnp.minimum(p, 120.0))))


def opacity(depth):
    k = LN2 * tau_scale
    small = depth * (k - depth * (k * k / 2))
    large = 1.0 - jnp.exp2(depth * -tau_scale)
    return jnp.where(depth < 2.5, small, large)


def pieces(value, count):
    result = []
    for _ in range(count):
        high = value.astype(bf16)
        result.append(high)
        value = value - high.astype(f32)
    return result


def fill_polynomials(coeffs, poly_ref):
    lane = lax.broadcasted_iota(jnp.int32, (8, 128), 1)
    tables = []
    for channel in range(4):
        terms = []
        for n in (1, 2, 3):
            high, low = (piece.astype(f32) for piece in pieces(coeffs[4 * channel + n] * (1.0 / LN2), 2))
            terms += [high, high, low, low]
        terms += [piece.astype(f32) for piece in pieces(coeffs[4 * channel] * (1.0 / LN2), 3)] + [jnp.zeros((8, 128), f32)]
        for tile in range(2):
            value = terms[8 * tile]
            for t in range(1, 8):
                value = jnp.where(lane // 16 == t, terms[8 * tile + t], value)
            tables.append(value)

    @pl.loop(0, 16)
    def _(cell):
        here = lane % 16 == cell
        for pair in range(2):
            rows = pl.ds(pl.multiple_of(cell * 32 + pair * 16, 16), 16)
            for tile in range(2):
                both = [jnp.where(here, tables[2 * (2 * pair + c) + tile], 0.0) for c in range(2)]
                poly_ref[rows, 128 * tile : 128 * (tile + 1)] = jnp.concatenate(both).astype(bf16)


def powers(s):
    result = []
    power = s
    for n in range(3):
        high, low = pieces(power, 2)
        result += [high, low, high, low]
        power = power * s
    return jnp.concatenate(result + [jnp.ones((64, 128), bf16)])


def shuffle(parts, place):
    group = lax.broadcasted_iota(jnp.int32, parts[0].shape, 1) // 32
    result = None
    for g in range(4):
        shift = (32 * (g - place)) % 128
        moved = pltpu.roll(parts[g], shift, 1) if shift else parts[g]
        result = moved if result is None else jnp.where(group == g, moved, result)
    return result


def kernel(
    coeff_hbm, index_hbm, spectrum_hbm, x_hbm, z_hbm,
    field_out, image_out,
    coeff_ref, index_ref, spectrum_ref, row_ref, class_ref, x_ref, z_ref, wave_ref, mode_ref, send_ref, recv_ref, pair_ref, poly_ref, even_ref, odd_ref, glow_ref, field_ref, light_ref, pack_ref, halo_ref, slab_ref,
    in_sem, x_sem, z_sem, send_sem, recv_sem, halo_send, halo_recv, slab_send, slab_recv,
):
    me = lax.axis_index("depth")
    plane = lax.axis_index("plane")
    planes = lax.axis_size("plane")
    next_plane = lax.rem(plane + 1, planes)
    last_plane = lax.rem(plane + planes - 1, planes)

    def half_of(step):
        return lax.rem(me // 4 + step, 2)

    def x_copy(step):
        half = half_of(step)
        return pltpu.make_async_copy(x_hbm.at[half], x_ref.at[half], x_sem.at[step])

    z_copy = pltpu.make_async_copy(z_hbm, z_ref, z_sem)
    spectrum_copy = pltpu.make_async_copy(spectrum_hbm, spectrum_ref, in_sem.at[0])
    small_copies = [
        pltpu.make_async_copy(coeff_hbm, coeff_ref, in_sem.at[1]),
        pltpu.make_async_copy(index_hbm, index_ref, in_sem.at[2]),
    ]
    spectrum_copy.start()

    for step in range(2):
        x_copy(step).start()

    z_copy.start()
    for copy in small_copies:
        copy.start()

    barrier = pltpu.get_barrier_semaphore()

    @pl.loop(1, 32)
    def _(step):
        pl.semaphore_signal(barrier, inc=1, device_id={"depth": lax.rem(me + step, 32)}, device_id_type=MESH)

    pl.semaphore_signal(barrier, inc=1, device_id={"plane": next_plane}, device_id_type=MESH)
    pl.semaphore_signal(barrier, inc=1, device_id={"plane": last_plane}, device_id_type=MESH)

    def mode_send(to):
        return pltpu.make_async_remote_copy(
            src_ref=send_ref.at[to], dst_ref=recv_ref.at[me], send_sem=send_sem.at[to], recv_sem=recv_sem.at[me],
            device_id={"depth": to}, device_id_type=MESH,
        )

    def mode_recv(source):
        return pltpu.make_async_remote_copy(
            src_ref=send_ref.at[source], dst_ref=recv_ref.at[source], send_sem=send_sem.at[source],
            recv_sem=recv_sem.at[source], device_id={"depth": source}, device_id_type=MESH,
        )

    def mode_keep():
        return pltpu.make_async_copy(send_ref.at[me], recv_ref.at[me], recv_sem.at[me])

    spectrum_copy.wait()
    row_ref[...] = spectrum_ref[...].reshape(256, NX)
    gather_classes(row_ref, class_ref)

    @pl.loop(0, 2)
    def _(step):
        half = half_of(step)
        x_copy(step).wait()
        for j in range(4):
            waves = dot(class_ref[j], x_ref[half, 0, j]) + dot(class_ref[j], x_ref[half, 1, j])
            wave_ref[j, 0] = waves[:128, :128] - waves[128:, 128:]
            wave_ref[j, 1] = waves[:128, 128:] + waves[128:, :128]
        for k in range(4):
            rows = slice(32 * k, 32 * k + 32)
            re = [wave_ref[j, 0, rows] for j in range(4)]
            im = [wave_ref[j, 1, rows] for j in range(4)]
            for i, pair in enumerate(residues(re, im)):
                mode_ref[i, 0, rows] = pair[0]
                mode_ref[i, 1, rows] = pair[1]

        @pl.when(step == 0)
        def _():
            pl.semaphore_wait(barrier, 33)

        @pl.loop(0, 4)
        def _(turn):
            i = lax.rem(me // 8 + turn + turn // 2 - 2 * (turn // 3), 4)
            first = 8 * i + 4 * half
            parts = [[] for _ in range(4)]
            for part in range(2):
                rows = [mode_ref[i, part, pl.ds(y, 32, stride=4), :] for y in range(4)]
                for d in range(4):
                    parts[d].append(shuffle(rows, d))
            for d in range(4):
                codes, level = encode(parts[d])
                send_ref[first + d, 0:32] = codes
                send_ref[first + d, 32:33] = level

            @pl.loop(0, 4)
            def _(d):
                to = first + d

                @pl.when(to != me)
                def _():
                    mode_send(to).start()

                @pl.when(to == me)
                def _():
                    mode_keep().start()

    for copy in small_copies:
        copy.wait()
    fill_polynomials(coefficients(coeff_ref, index_ref), poly_ref)

    @pl.loop(0, 8)
    def _(s):
        @pl.loop(0, 4)
        def _(j):
            source = s + 8 * j

            @pl.when(source != me)
            def _():
                mode_recv(source).wait_recv()

            @pl.when(source == me)
            def _():
                mode_keep().wait()

        re, im = [], []
        for j in range(4):
            real, imag = decode(recv_ref[s + 8 * j, 0:32], recv_ref[s + 8 * j, 32:33])
            re.append(real)
            im.append(imag)
        for r, pair in enumerate(residues(re, im)):
            for part in range(2):
                high, low = split(pair[part])
                rows = pl.ds(pl.multiple_of(part * 256 + s * 32, 32), 32)
                pair_ref[r, rows, 0:128] = high
                pair_ref[r, rows, 128:256] = low

    z_copy.wait()

    for r in range(4):
        p = dot(z_ref[r], pair_ref[r])
        field_ref[r] = (p[:256, :128] + p[:256, 128:]) + (p[256:, :128] + p[256:, 128:])

    @pl.loop(0, 4)
    def _(step):
        rows = pl.ds(pl.multiple_of(step * 64, 64), 64)
        parts = [field_ref[r, rows, :] for r in range(4)]
        pack_ref[0, rows, :] = shuffle(parts, 3)
        pack_ref[1, rows, :] = shuffle(parts, 0)

    halos = [
        pltpu.make_async_remote_copy(
            src_ref=pack_ref.at[side], dst_ref=halo_ref.at[side], send_sem=halo_send.at[side],
            recv_sem=halo_recv.at[side], device_id={"plane": to}, device_id_type=MESH,
        )
        for side, to in ((0, next_plane), (1, last_plane))
    ]
    for halo in halos:
        halo.start()

    def own_rows(slab):
        return field_ref.at[:, pl.ds(pl.multiple_of(slab * 8, 8), 8), :]

    def slab_send_copy(to):
        return pltpu.make_async_remote_copy(
            src_ref=own_rows(to), dst_ref=slab_ref.at[me], send_sem=slab_send.at[to], recv_sem=slab_recv.at[me],
            device_id={"depth": to}, device_id_type=MESH,
        )

    def slab_recv_copy(source):
        return pltpu.make_async_remote_copy(
            src_ref=own_rows(source), dst_ref=slab_ref.at[source], send_sem=slab_send.at[source],
            recv_sem=slab_recv.at[source], device_id={"depth": source}, device_id_type=MESH,
        )

    slab_keep = pltpu.make_async_copy(own_rows(me), slab_ref.at[me], slab_recv.at[me])

    slab_keep.start()

    @pl.loop(1, 32)
    def _(step):
        slab_send_copy(lax.rem(me + step, 32)).start()

    def evaluate(block, to_ref):
        rows = pl.ds(pl.multiple_of(jnp.minimum(block, 15) * 16, 16), 16)
        for pair in range(2):
            factors = [powers(field_ref[2 * pair + c, rows, :]) for c in range(2)]
            to_ref[pair] = dot(poly_ref[...], jnp.concatenate(factors, axis=1))

    def cell_depths(from_ref, r, k, channel):
        first = 32 * k + 8 * channel
        return softplus(from_ref[r // 2, first : first + 8, 128 * (r % 2) : 128 * (r % 2) + 128])

    def cell_light(block, r, k):
        rows = pl.ds(pl.multiple_of(block * 16, 16), 16)
        return jnp.broadcast_to(light_ref[r, rows, :][k : k + 1, :], (8, 128))

    def absorb(from_ref, r, k, through):
        weight = through * opacity(cell_depths(from_ref, r, k, 3))
        return weight, through - weight

    def join_slabs(g):
        for r in range(4):
            parts = [slab_ref[g * 4 + d, r] for d in range(4)]
            for y in range(4):
                field_out[pl.ds(r * 32 + g * 4 + y, 8, stride=128), :] = shuffle(parts, y)

    def in_fours(start, cells, join):
        def step(n, state):
            block = start + 4 * n
            groups = [lax.rem(me // 4 + 15 - k, 8) for k in range(8)] if join else []
            for g in groups:

                @pl.loop(0, 4)
                def _(d):
                    source = 4 * g + d

                    @pl.when(source != me)
                    def _():
                        slab_recv_copy(source).wait_recv()

                    @pl.when(source == me)
                    def _():
                        slab_keep.wait()

            for k in range(4):
                here, ahead = (even_ref, odd_ref) if k % 2 == 0 else (odd_ref, even_ref)
                evaluate(block + k + 1, ahead)
                state = cells(block + k, here, state)
                for g in groups[2 * k : 2 * k + 2]:
                    join_slabs(g)
            return state

        return step

    def front(block, from_ref, state):
        through = state
        for k in range(16):
            for r in range(4):
                weight, through = absorb(from_ref, r, k, through)
                for j in range(3):
                    glow_ref[block, 4 * k + r, j] = weight * cell_depths(from_ref, r, k, j)
        return through

    zero = jnp.zeros((8, 128), f32)
    evaluate(0, even_ref)
    through = lax.fori_loop(0, 3, in_fours(0, front, False), zero + 1.0)

    for halo in halos:
        halo.wait_recv()

    @pl.loop(0, 4)
    def _(step):
        rows = pl.ds(pl.multiple_of(step * 64, 64), 64)
        for r in range(4):
            light_ref[r, rows, :] = lighting(field_ref[r, rows, :], halo_ref[0, rows, :], halo_ref[1, rows, :], r)

    def lit(block, colors):
        colors = list(colors)
        for k in range(16):
            for r in range(4):
                light = cell_light(block, r, k)
                for j in range(3):
                    n = j + 3 * (r % 2)
                    colors[n] = colors[n] + light * glow_ref[block, 4 * k + r, j]
        return tuple(colors)

    colors = lax.fori_loop(0, 12, lit, (zero,) * 6)
    colors = [colors[j] + colors[j + 3] for j in range(3)]

    def back(block, from_ref, state):
        *colors, through = state
        for k in range(16):
            for r in range(4):
                weight, through = absorb(from_ref, r, k, through)
                weight = weight * cell_light(block, r, k)
                for j in range(3):
                    colors[j] = colors[j] + weight * cell_depths(from_ref, r, k, j)
        return (*colors, through)

    *colors, through = in_fours(12, back, True)(0, (*colors, through))
    for channel, image in enumerate([color * LN2 for color in colors] + [through]):
        for y in range(4):
            moved = pltpu.roll(image, 128 - 32 * y, 1) if y else image
            image_out[pl.ds(channel * 4 + y, 8, stride=16), :] = moved

    @pl.loop(1, 32)
    def _(step):
        to = lax.rem(me + step, 32)
        mode_send(to).wait_send()
        slab_send_copy(to).wait_send()

    for halo in halos:
        halo.wait_send()


def body(x_tab, z_tab, spectrum, transfer_coeffs, transfer_index):
    vmem = pl.BlockSpec(memory_space=pltpu.VMEM)
    hbm = pl.BlockSpec(memory_space=pl.ANY)
    sem = pltpu.SemaphoreType.DMA
    field, image = pl.pallas_call(
        kernel,
        out_shape=[jax.ShapeDtypeStruct((1024, 128), f32), jax.ShapeDtypeStruct((128, 128), f32)],
        in_specs=[hbm] * 5,
        out_specs=[vmem, vmem],
        scratch_shapes=[
            pltpu.SMEM((4, 4, 8), f32),
            pltpu.SMEM((8,), jnp.int32),
            pltpu.VMEM((2, 32, 4, NX), bf16),
            pltpu.VMEM((256, NX), bf16),
            pltpu.VMEM((4, 256, 256), bf16),
            pltpu.VMEM((2, 2, 4, 256, 256), bf16),
            pltpu.VMEM((4, 512, 512), bf16),
            pltpu.VMEM((4, 2, 128, 128), f32),
            pltpu.VMEM((4, 2, 128, 128), f32),
            pltpu.VMEM((32, 33, 128), jnp.int32),
            pltpu.VMEM((32, 33, 128), jnp.int32),
            pltpu.VMEM((4, 512, 256), bf16),
            pltpu.VMEM((512, 256), bf16),
            pltpu.VMEM((2, 512, 256), f32),
            pltpu.VMEM((2, 512, 256), f32),
            pltpu.VMEM((12, 64, 3, 8, 128), f32),
            pltpu.VMEM((4, 256, 128), f32),
            pltpu.VMEM((4, 256, 128), f32),
            pltpu.VMEM((2, 256, 128), f32),
            pltpu.VMEM((2, 256, 128), f32),
            pltpu.VMEM((32, 4, 8, 128), f32),
            sem((3,)), sem((2,)), sem, sem((32,)), sem((32,)), sem((2,)), sem((2,)), sem((32,)), sem((32,)),
        ],
        compiler_params=pltpu.CompilerParams(
            collective_id=0, has_side_effects=True, vmem_limit_bytes=53 * 2**20
        ),
    )(transfer_coeffs.transpose(1, 2, 0), transfer_index, spectrum, x_tab, z_tab)
    scalar_field = field.reshape(32, 8, 4, 128).transpose(0, 2, 1, 3).reshape(32, 4, NX)
    rendered = image[:, :32].reshape(8, 4, 4, 32)
    return scalar_field, rendered


def solution(mesh):
    x_tab, z_tab = x_table(), z_table()
    mapped = jax.shard_map(
        body,
        mesh=mesh,
        in_specs=(P(), P(), P(None, "depth", "plane", None), P(), P()),
        out_specs=(P("depth", "plane", None), P(None, None, "plane", "depth")),
        check_vma=False,
    )

    def run(spectrum, transfer_coeffs, transfer_index):
        return mapped(x_tab, z_tab, spectrum, transfer_coeffs, transfer_index)

    return run
```
